32 devices in a mesh: tile: 8 (over y, x, core), lev: 4 (over z).
Axes of the slice: x: 2, y: 2, z: 4, core: 2. Of those that a mesh axis runs over, the one named last changes fastest.
Arguments:
- conc: float32 [8, 4, 16, 4, 4096], P('tile', None, None, 'lev'), may hold values from 0 to 2
- wind_u: float32 [8, 4, 4096], P('tile', 'lev'), may hold values from 0.02 to 0.2
- wind_v: float32 [8, 4, 4096], P('tile', 'lev'), may hold values from 0.02 to 0.2
- emission: float32 [8, 4096], P('tile'), may hold values from 0.01 to 1
- member_rate: float32 [4, 16], replicated, may hold values from 0.1 to 2
- column_top: int32 [4], replicated, may hold values from 1 to 4
- settle_rate: float32 [16, 4], replicated, may hold values from 0.5 to 30
- neighbours: int32 [8, 4], replicated, may hold values from -1 to 7, as said below
Outputs:
- final_conc: float32 [8, 4, 16, 4, 4096], P('tile', None, None, 'lev')
The draws below stay inside these ranges and needn't reach their ends.
Inputs may be any that keep to these rules, and one draw needn't show every extreme that they name: Tiles form a grid 8 tiles wide; each tile's entries name its grid neighbours, and a tile named as some tile's east neighbour names that tile as its west neighbour (likewise south and north).
All inputs are finite; a program needn't handle non-finite values.
Results may differ from the reference program's by a relative error of at most 0.0001.
Values sent between devices are 32-bit elements; how exact they have to be, the bound alone decides.
A program may use at most 64 MiB of HBM per device.

```python
import math
import jax
import jax.numpy as jnp
from jax import lax

TS = 64
M = 4
B = 16
STEPS = 6
C = 4096
NT = 8
NZ = 4


def draw_neighbours(key, part):
    position = jax.random.permutation(key, NT).astype(jnp.int32)
    owner = jnp.argsort(position).astype(jnp.int32)
    row_count = NT // 8
    row_at = position // 8
    column_at = position % 8
    west = jnp.where(column_at > 0, owner[jnp.clip(position - 1, 0, NT - 1)], -1)
    east = jnp.where(column_at < 7, owner[jnp.clip(position + 1, 0, NT - 1)], -1)
    south = jnp.where(row_at > 0, owner[jnp.clip(position - 8, 0, NT - 1)], -1)
    north = jnp.where(row_at < row_count - 1, owner[jnp.clip(position + 8, 0, NT - 1)], -1)
    return jnp.stack([west, east, south, north], axis=1).astype(jnp.int32)


def plant(result, rng, low, top_value):
    extent = result.shape
    index_at = [jax.random.randint(jax.random.fold_in(rng, axis), (), 0, extent[axis]) for axis in range(len(extent))]
    result = result.at[tuple(index_at)].set(low)
    longest = extent.index(max(extent))
    index_at[longest] = (index_at[longest] + 1) % extent[longest]
    return result.at[tuple(index_at)].set(top_value)


def steps_of(own_key, shape, split, least, top_value):
    def one(axis_at, parts):
        steps = jax.random.uniform(jax.random.fold_in(jax.random.fold_in(own_key, 6), axis_at), (parts,), jnp.float32, least / len(split), top_value / len(split))
        return jnp.repeat(jnp.exp(steps), shape[axis_at] // parts).reshape((-1,) + (1,) * (len(shape) - axis_at - 1))

    gain = one(*split[0])
    for cut in split[1:]:
        gain = gain * one(*cut)
    return gain


def setup_inputs(seed: int = 0) -> dict:
    key_of = jax.random.split(jax.random.key(seed), 9)
    return {
        "conc": jnp.clip(2.0 * jax.random.uniform(key_of[0], (NT, M, B, NZ, C), jnp.float32) ** steps_of(key_of[0], (NT, M, B, NZ, C), ((0, 8), (3, 4)), -0.2, 0.2), 0.0, 2.0),
        "wind_u": jnp.clip(jnp.exp(math.log(0.2) - 2.3025851 * jax.random.uniform(key_of[1], (NT, NZ, C), jnp.float32) ** steps_of(key_of[1], (NT, NZ, C), ((0, 8), (1, 4)), -0.2, 0.2)), 0.02, 0.2),
        "wind_v": jnp.clip(jnp.exp(math.log(0.2) - 2.3025851 * jax.random.uniform(key_of[2], (NT, NZ, C), jnp.float32) ** steps_of(key_of[2], (NT, NZ, C), ((0, 8), (1, 4)), -0.2, 0.2)), 0.02, 0.2),
        "emission": jnp.clip(jnp.exp(math.log(1.0) - 4.6051702 * jax.random.uniform(key_of[3], (NT, C), jnp.float32) ** steps_of(key_of[3], (NT, C), ((0, 8),), -0.2, 0.2)), 0.01, 1.0),
        "member_rate": jnp.clip(jnp.exp(jax.random.uniform(key_of[4], (M, B), jnp.float32, math.log(0.1), math.log(2.0))), 0.1, 2.0),
        "column_top": plant(jax.random.randint(key_of[5], (M,), 1, NZ + 1), jax.random.fold_in(key_of[5], 1), 1, NZ).astype(jnp.int32),
        "settle_rate": jnp.clip(jnp.exp(jax.random.uniform(key_of[6], (B, NZ), jnp.float32, math.log(0.5), math.log(30.0))), 0.5, 30.0),
        "neighbours": draw_neighbours(jax.random.fold_in(key_of[8], 71), 0),
    }


def make_inverse(settle_rate):
    levels = settle_rate.shape[1]
    ident = jnp.eye(levels, dtype=settle_rate.dtype)
    diag_all = 1.0 + settle_rate
    next_rate = jnp.concatenate([settle_rate[:, 1:], jnp.zeros_like(settle_rate[:, :1])], axis=1)

    def back_step(carry, inputs):
        unit_row, rate_next, diag_here = inputs
        row_now = (unit_row[None, :] + rate_next[:, None] * carry) / diag_here[:, None]
        return row_now, row_now

    start = jnp.zeros((settle_rate.shape[0], levels), dtype=settle_rate.dtype)
    unused, stacked = lax.scan(back_step, start, (ident, next_rate.T, diag_all.T), reverse=True)
    return jnp.transpose(stacked, (1, 0, 2))


def pick_face(faces, index):
    chosen = faces[jnp.clip(index, 0, faces.shape[0] - 1)]
    valid = (index >= 0).astype(jnp.float32)
    return chosen * valid[:, None, None, None, None]


def horizontal(field, wind_u, wind_v, neighbours):
    tiles, members, bins, levels, cells = field.shape
    cells_grid = field.reshape(tiles, members, bins, levels, TS, TS)
    west_face = cells_grid[..., :, 0]
    east_face = cells_grid[..., :, TS - 1]
    south_face = cells_grid[..., 0, :]
    north_face = cells_grid[..., TS - 1, :]
    ghost_west = pick_face(east_face, neighbours[:, 0])
    ghost_east = pick_face(west_face, neighbours[:, 1])
    ghost_south = pick_face(north_face, neighbours[:, 2])
    ghost_north = pick_face(south_face, neighbours[:, 3])
    from_west = jnp.concatenate([ghost_west[..., :, None], cells_grid[..., :, :-1]], axis=-1)
    from_east = jnp.concatenate([cells_grid[..., :, 1:], ghost_east[..., :, None]], axis=-1)
    from_south = jnp.concatenate([ghost_south[..., None, :], cells_grid[..., :-1, :]], axis=-2)
    from_north = jnp.concatenate([cells_grid[..., 1:, :], ghost_north[..., None, :]], axis=-2)
    speed_u = wind_u.reshape(tiles, 1, 1, levels, TS, TS)
    speed_v = wind_v.reshape(tiles, 1, 1, levels, TS, TS)
    moved = cells_grid + 0.15 * (from_west + from_east + from_south + from_north - 4.0 * cells_grid)
    moved = moved - speed_u * (cells_grid - from_west) - speed_v * (cells_grid - from_south)
    return moved.reshape(tiles, members, bins, levels, cells)


def reference(conc, wind_u, wind_v, emission, member_rate, column_top, settle_rate, neighbours):
    levels = conc.shape[3]
    below = (jnp.arange(levels, dtype=jnp.int32)[None, :] < column_top[:, None]).astype(jnp.float32)
    source = emission[:, None, None, None, :] * member_rate[None, :, :, None, None] * below[None, :, None, :, None]
    inverse = make_inverse(settle_rate)
    field = conc
    for turn_index in range(STEPS):
        field = field + source
        moved = horizontal(field, wind_u, wind_v, neighbours)
        field = jnp.einsum("bkj,tmbjc->tmbkc", inverse, moved, precision=lax.Precision.HIGHEST)
    return field
```

```python
import functools
import jax
import jax.numpy as jnp
from jax import lax
from jax.experimental import pallas as pl
from jax.experimental.pallas import tpu as pltpu
from jax.sharding import PartitionSpec as P

TS = 64
STEPS = 6


def make_inverse(settle_rate):
    levels = settle_rate.shape[1]
    ident = jnp.eye(levels, dtype=settle_rate.dtype)
    diag_all = 1.0 + settle_rate
    next_rate = jnp.concatenate([settle_rate[:, 1:], jnp.zeros_like(settle_rate[:, :1])], axis=1)

    def back_step(carry, inputs):
        unit_row, rate_next, diag_here = inputs
        row_now = (unit_row[None, :] + rate_next[:, None] * carry) / diag_here[:, None]
        return (row_now, row_now)

    start = jnp.zeros((settle_rate.shape[0], levels), dtype=settle_rate.dtype)
    unused, stacked = lax.scan(back_step, start, (ident, next_rate.T, diag_all.T), reverse=True)
    return jnp.transpose(stacked, (1, 0, 2))


def pick_face(all_faces, index, which):
    chosen = all_faces[jnp.clip(index, 0, all_faces.shape[0] - 1), which]
    valid = (index >= 0).astype(jnp.float32)
    return chosen * valid[:, None, None, None, None]


def horizontal(field, speed_u, speed_v, own_lists):
    per_tile, members, bins, levels, cells = field.shape
    side = TS
    west_face = field[..., 0::side]
    east_face = field[..., side - 1 :: side]
    south_face = field[..., :side]
    north_face = field[..., cells - side :]
    edge_stack = jnp.stack([west_face, east_face, south_face, north_face], axis=1)
    edge_flat = edge_stack.reshape(per_tile, 4, members, bins, levels * side)
    gathered = lax.all_gather(edge_flat, "tile", axis=0, tiled=True)
    all_faces = gathered.reshape(gathered.shape[0], 4, members, bins, levels, side)
    ghost_west = pick_face(all_faces, own_lists[:, 0], 1)
    ghost_east = pick_face(all_faces, own_lists[:, 1], 0)
    ghost_south = pick_face(all_faces, own_lists[:, 2], 3)
    ghost_north = pick_face(all_faces, own_lists[:, 3], 2)
    column_of = jnp.arange(cells, dtype=jnp.int32) % side
    shifted_right = jnp.concatenate([field[..., :1], field[..., :-1]], axis=-1)
    shifted_left = jnp.concatenate([field[..., 1:], field[..., -1:]], axis=-1)
    from_west = jnp.where(column_of == 0, jnp.repeat(ghost_west, side, axis=-1), shifted_right)
    from_east = jnp.where(
        column_of == side - 1, jnp.repeat(ghost_east, side, axis=-1), shifted_left
    )
    from_south = jnp.concatenate([ghost_south, field[..., : cells - side]], axis=-1)
    from_north = jnp.concatenate([field[..., side:], ghost_north], axis=-1)
    moved = field + 0.15 * (from_west + from_east + from_south + from_north - 4.0 * field)
    moved = moved - speed_u * (field - from_west) - speed_v * (field - from_south)
    return moved


def per_device(conc, wind_u, wind_v, emission, member_rate, column_top, settle_rate, neighbours):
    per_tile, members, bins, level_count, cells = conc.shape
    own_lists = lax.dynamic_slice_in_dim(neighbours, lax.axis_index("tile") * per_tile, per_tile, 0)
    inverse = make_inverse(settle_rate)
    levels_here = lax.axis_index("lev") * level_count + jnp.arange(level_count, dtype=jnp.int32)
    below = (levels_here[None, :] < column_top[:, None]).astype(jnp.float32)
    source = (
        emission[:, None, None, None, :]
        * member_rate[None, :, :, None, None]
        * below[None, :, None, :, None]
    )
    speed_u = wind_u.reshape(per_tile, 1, 1, level_count, cells)
    speed_v = wind_v.reshape(per_tile, 1, 1, level_count, cells)
    field = conc
    for turn_index in range(STEPS):
        field = field + source
        moved = horizontal(field, speed_u, speed_v, own_lists)
        columns = lax.all_to_all(moved, "lev", split_axis=4, concat_axis=3, tiled=True)
        settled = jnp.einsum("bkj,tmbjc->tmbkc", inverse, columns, precision=lax.Precision.HIGHEST)
        field = lax.all_to_all(settled, "lev", split_axis=3, concat_axis=4, tiled=True)
    return field


GRID_WIDTH = 8
HALO = 8
GROUP = 4


def lane_of(shape):
    return lax.broadcasted_iota(jnp.int32, shape, 1)


def pack_edges(tiles):
    group = ((lane_of(tiles[0].shape) + HALO) // (2 * HALO)) % GROUP
    packed = tiles[0]
    for i in range(1, len(tiles)):
        packed = jnp.where(group == i, pltpu.roll(tiles[i], 2 * HALO * i, 1), packed)
    return packed


def spread(main, edges, i):
    own = lane_of(main.shape) < TS
    turned = edges if i == 0 else pltpu.roll(edges, 128 - 2 * HALO * i, 1)
    even = jnp.where(own, main, pltpu.roll(turned, TS, 1))
    odd = jnp.where(own, pltpu.roll(main, TS, 1), turned)
    return even, odd


def window_kernel(
    tiles, levs, members,
    rate_ref, top_ref, settle_ref, near_ref, x_ref, u_ref, v_ref, em_ref,
    out_ref,
    inbuf, wind, em, halo, whalo, pick, eo, coef, emx, outbuf, solve,
    in_send, in_recv, wind_send, wind_recv, em_sem, whalo_send, whalo_recv, halo_send, halo_recv, out_send, out_recv,
):
    t = lax.axis_index("tile")
    d = lax.axis_index("lev")
    lev_peers = [lax.rem(d + o, levs) for o in range(1, levs)]
    tile_peers = [lax.rem(t + o, tiles) for o in range(1, tiles)]
    shape = (TS // 2, 128)

    barrier = pltpu.get_barrier_semaphore()
    for p in lev_peers:
        pl.semaphore_signal(barrier, inc=1, device_id={"lev": p})
    for p in tile_peers:
        pl.semaphore_signal(barrier, inc=1, device_id={"tile": p})
    pl.semaphore_wait(barrier, len(lev_peers) + len(tile_peers))

    def remote(src, dst, send_sem, recv_sem, where):
        return pltpu.make_async_remote_copy(
            src_ref=src, dst_ref=dst, send_sem=send_sem, recv_sem=recv_sem, device_id=where
        )

    def mine(p):
        return pl.ds(p * GROUP, GROUP)

    def wind_copy(w, p, slot):
        return remote((u_ref, v_ref)[w], wind.at[w, slot], wind_send.at[w, p], wind_recv.at[w, slot], {"lev": p})

    def in_copy(c, p, slot):
        return remote(x_ref.at[c, mine(p)], inbuf.at[c, slot], in_send.at[c, p], in_recv.at[c, slot], {"lev": p})

    def out_copy(c, p, slot):
        return remote(
            outbuf.at[c, p], out_ref.at[c, mine(slot)], out_send.at[c, p], out_recv.at[c, slot], {"lev": p}
        )

    def wind_edge_copy(p, slot):
        return remote(whalo.at[t], whalo.at[slot], whalo_send.at[p], whalo_recv.at[slot], {"tile": p})

    def edge_copy(c, p, slot):
        return remote(halo.at[c, t], halo.at[c, slot], halo_send.at[c, p], halo_recv.at[c, slot], {"tile": p})

    def own_wind(w):
        return pltpu.make_async_copy((u_ref, v_ref)[w], wind.at[w, d], wind_recv.at[w, d])

    def own_in(c):
        return pltpu.make_async_copy(x_ref.at[c, mine(d)], inbuf.at[c, d], in_recv.at[c, d])

    def own_out(c):
        return pltpu.make_async_copy(outbuf.at[c, d], out_ref.at[c, mine(d)], out_recv.at[c, d])

    def start_in(c):
        for p in lev_peers:
            in_copy(c, p, d).start()
        own_in(c).start()

    for w in range(2):
        for p in lev_peers:
            wind_copy(w, p, d).start()
        own_wind(w).start()
    own_em = pltpu.make_async_copy(em_ref, em, em_sem)
    own_em.start()
    start_in(0)
    start_in(1)

    for i in range(GROUP):
        for k in range(levs):
            q = 1.0 / (1.0 + jnp.full((8, 128), settle_ref[k, d * GROUP + i], jnp.float32))
            solve[i, k, 0] = q
            if k + 1 < levs:
                solve[i, k, 1] = q * settle_ref[k + 1, d * GROUP + i]
            else:
                solve[i, k, 1] = jnp.zeros((8, 128), jnp.float32)

    lane = lane_of(shape)
    row = lax.broadcasted_iota(jnp.int32, shape, 0)
    west, east = near_ref[0, t], near_ref[1, t]
    has_west = jnp.where(west >= 0, 1.0, 0.0)
    has_east = jnp.where(east >= 0, 1.0, 0.0)
    east_lane = lax.rem(lane_of((8, 128)), 2 * HALO) < HALO
    for p in range(tiles):
        pick[p] = jnp.where(
            east_lane,
            jnp.full((8, 128), jnp.where(east == p, 1.0, 0.0), jnp.float32),
            jnp.full((8, 128), jnp.where(west == p, 1.0, 0.0), jnp.float32),
        )

    def wide(value):
        return jnp.concatenate([value] * (shape[0] // 8), axis=0)

    def edges_of(packed):
        total = wide(pick[0]) * packed(0)
        for p in range(1, tiles):
            total = total + wide(pick[p]) * packed(p)
        return total

    own_em.wait()
    for w in range(2):
        own_wind(w).wait()
        for p in lev_peers:
            wind_copy(w, p, p).wait_recv()
    for w in range(2):
        whalo[t, w] = pack_edges([wind[w, k] for k in range(levs)])
    whalo[t, 2] = em[...]
    for p in tile_peers:
        wind_edge_copy(p, t).start()

    def gather_edges(c):
        own_in(c).wait()
        for p in lev_peers:
            in_copy(c, p, p).wait_recv()

        @pl.when(c + 2 < members)
        def _():
            start_in(c + 2)

        def pack_level(k, carry):
            halo[c, t, k] = pack_edges([inbuf[c, k, i] for i in range(GROUP)])
            return carry

        lax.fori_loop(0, levs, pack_level, 0)
        for p in tile_peers:
            edge_copy(c, p, t).start()

    def coefficients():
        for p in tile_peers:
            wind_edge_copy(p, p).wait_recv()
        live = jnp.where(lane < TS, 1.0, 0.0)
        live = jnp.where((lane >= TS) & (lane < TS + HALO), has_east, live)
        live = jnp.where(lane >= 128 - HALO, has_west, live)
        edges = [edges_of(lambda p, w=w: whalo[p, w]) for w in range(3)]
        even, odd = spread(em[...], edges[2], 0)
        emx[0] = even * live
        emx[1] = odd * live
        emx[2] = 0.15 * live
        emx[3] = jnp.where(row == TS // 2 - 1, 0.0, 0.15 * live)
        for k in range(levs):
            us = spread(wind[0, k], edges[0], k)
            vs = spread(wind[1, k], edges[1], k)
            for e in range(2):
                coef[k, e, 0] = (0.4 - us[e] - vs[e]) * live
                coef[k, e, 1] = (0.15 + us[e]) * live
                south = (0.15 + vs[e]) * live
                coef[k, e, 2] = jnp.where(row == 0, 0.0, south) if e == 0 else south

    def run(c):
        for p in tile_peers:
            edge_copy(c, p, p).wait_recv()

        def build(k, carry):
            edges = edges_of(lambda p: halo[c, p, k])
            for i in range(GROUP):
                even, odd = spread(inbuf[c, k, i], edges, i)
                eo[k, i, 0] = even
                eo[k, i, 1] = odd
            return carry

        lax.fori_loop(0, levs, build, 0)

        def one_bin(i, carry):
            rate = rate_ref[c, d * GROUP + i]
            above_even = above_odd = None
            for k in reversed(range(levs)):
                s = jnp.where(k < top_ref[c], rate, 0.0)
                even = eo[k, i, 0] + emx[0] * s
                odd = eo[k, i, 1] + emx[1] * s
                moved_even = (
                    coef[k, 0, 0] * even
                    + coef[k, 0, 1] * pltpu.roll(even, 1, 1)
                    + coef[k, 0, 2] * pltpu.roll(odd, 1, 0)
                    + emx[2] * (pltpu.roll(even, 127, 1) + odd)
                )
                moved_odd = (
                    coef[k, 1, 0] * odd
                    + coef[k, 1, 1] * pltpu.roll(odd, 1, 1)
                    + coef[k, 1, 2] * even
                    + emx[2] * pltpu.roll(odd, 127, 1)
                    + emx[3] * pltpu.roll(even, shape[0] - 1, 0)
                )
                q = wide(solve[i, k, 0])
                new_even, new_odd = q * moved_even, q * moved_odd
                if above_even is not None:
                    g = wide(solve[i, k, 1])
                    new_even = new_even + g * above_even
                    new_odd = new_odd + g * above_odd
                eo[k, i, 0] = new_even
                eo[k, i, 1] = new_odd
                above_even, above_odd = new_even, new_odd
            return carry

        def one_step(step, carry):
            return lax.fori_loop(0, GROUP, one_bin, carry, unroll=2)

        lax.fori_loop(0, STEPS, one_step, 0)

        def join(k, carry):
            for i in range(GROUP):
                outbuf[c, k, i] = jnp.where(lane < TS, eo[k, i, 0], pltpu.roll(eo[k, i, 1], TS, 1))
            return carry

        lax.fori_loop(0, levs, join, 0)
        for p in lev_peers:
            out_copy(c, p, d).start()
        own_out(c).start()

    gather_edges(0)
    coefficients()

    def one_member(c, carry):
        @pl.when(c + 1 < members)
        def _():
            gather_edges(c + 1)

        run(c)
        return carry

    lax.fori_loop(0, members, one_member, 0)

    def finish(c, carry):
        own_out(c).wait()
        for p in lev_peers:
            out_copy(c, p, p).wait_recv()
            out_copy(c, p, d).wait_send()
            in_copy(c, p, d).wait_send()
        for p in tile_peers:
            edge_copy(c, p, t).wait_send()
        return carry

    for w in range(2):
        for p in lev_peers:
            wind_copy(w, p, d).wait_send()
    for p in tile_peers:
        wind_edge_copy(p, t).wait_send()
    lax.fori_loop(0, members, finish, 0)


def window(tiles, levs, conc, wind_u, wind_v, emission, member_rate, column_top, settle_rate, neighbours):
    members, bins = conc.shape[1], conc.shape[2]
    tile = (TS // 2, 128)
    x = conc.reshape((members, bins) + tile)
    f32 = jnp.float32
    dma = pltpu.SemaphoreType.DMA
    smem = pl.BlockSpec(memory_space=pltpu.SMEM)
    hbm = pl.BlockSpec(memory_space=pltpu.HBM)
    anywhere = pl.BlockSpec(memory_space=pl.ANY)
    out = pl.pallas_call(
        functools.partial(window_kernel, tiles, levs, members),
        out_shape=pltpu.VMEM(x.shape, f32),
        in_specs=[smem] * 4 + [hbm] * 4,
        out_specs=pl.BlockSpec(memory_space=pltpu.VMEM),
        scratch_shapes=[
            pltpu.VMEM((members, levs, GROUP) + tile, f32),
            pltpu.VMEM((2, levs) + tile, f32),
            pltpu.VMEM(tile, f32),
            pltpu.VMEM((members, tiles, levs) + tile, f32),
            pltpu.VMEM((tiles, 3) + tile, f32),
            pltpu.VMEM((tiles, 8, 128), f32),
            pltpu.VMEM((levs, GROUP, 2) + tile, f32),
            pltpu.VMEM((levs, 2, 3) + tile, f32),
            pltpu.VMEM((4,) + tile, f32),
            pltpu.VMEM((members, levs, GROUP) + tile, f32),
            pltpu.VMEM((GROUP, levs, 2, 8, 128), f32),
            dma((members, levs)),
            dma((members, levs)),
            dma((2, levs)),
            dma((2, levs)),
            dma,
            dma((tiles,)),
            dma((tiles,)),
            dma((members, tiles)),
            dma((members, tiles)),
            dma((members, levs)),
            dma((members, levs)),
        ],
        compiler_params=pltpu.CompilerParams(
            collective_id=0, has_side_effects=True, vmem_limit_bytes=58 * 1024 * 1024
        ),
        name="window",
    )(
        member_rate, column_top, settle_rate.T, neighbours.T,
        x, wind_u.reshape(tile), wind_v.reshape(tile), emission.reshape(tile),
    )
    return out.reshape(conc.shape)


def choose(mesh):
    tiles, levs = mesh.shape["tile"], mesh.shape["lev"]

    def body(conc, *rest):
        per_tile, members, bins, level_count, cells = conc.shape
        one_row = tiles * per_tile == GRID_WIDTH
        fits = per_tile == 1 and level_count == 1 and bins == levs * GROUP and levs <= GROUP and members > 1
        if one_row and fits and cells == TS * TS and TS == 64 and STEPS <= HALO:
            return window(tiles, levs, conc, *rest)
        return per_device(conc, *rest)

    return body


def solution(mesh):
    return jax.shard_map(
        choose(mesh),
        mesh=mesh,
        in_specs=(
            P("tile", None, None, "lev", None),
            P("tile", "lev", None),
            P("tile", "lev", None),
            P("tile", None),
            P(),
            P(),
            P(),
            P(),
        ),
        out_specs=P("tile", None, None, "lev", None),
        check_vma=False,
    )
```

```python
import functools
import jax
import jax.numpy as jnp
from jax import lax
from jax.experimental import pallas as pl
from jax.experimental.pallas import tpu as pltpu
from jax.sharding import PartitionSpec as P

TS = 64
STEPS = 6


def make_inverse(settle_rate):
    levels = settle_rate.shape[1]
    ident = jnp.eye(levels, dtype=settle_rate.dtype)
    diag_all = 1.0 + settle_rate
    next_rate = jnp.concatenate([settle_rate[:, 1:], jnp.zeros_like(settle_rate[:, :1])], axis=1)

    def back_step(carry, inputs):
        unit_row, rate_next, diag_here = inputs
        row_now = (unit_row[None, :] + rate_next[:, None] * carry) / diag_here[:, None]
        return (row_now, row_now)

    start = jnp.zeros((settle_rate.shape[0], levels), dtype=settle_rate.dtype)
    unused, stacked = lax.scan(back_step, start, (ident, next_rate.T, diag_all.T), reverse=True)
    return jnp.transpose(stacked, (1, 0, 2))


def pick_face(all_faces, index, which):
    chosen = all_faces[jnp.clip(index, 0, all_faces.shape[0] - 1), which]
    valid = (index >= 0).astype(jnp.float32)
    return chosen * valid[:, None, None, None, None]


def horizontal(field, speed_u, speed_v, own_lists):
    per_tile, members, bins, levels, cells = field.shape
    side = TS
    west_face = field[..., 0::side]
    east_face = field[..., side - 1 :: side]
    south_face = field[..., :side]
    north_face = field[..., cells - side :]
    edge_stack = jnp.stack([west_face, east_face, south_face, north_face], axis=1)
    edge_flat = edge_stack.reshape(per_tile, 4, members, bins, levels * side)
    gathered = lax.all_gather(edge_flat, "tile", axis=0, tiled=True)
    all_faces = gathered.reshape(gathered.shape[0], 4, members, bins, levels, side)
    ghost_west = pick_face(all_faces, own_lists[:, 0], 1)
    ghost_east = pick_face(all_faces, own_lists[:, 1], 0)
    ghost_south = pick_face(all_faces, own_lists[:, 2], 3)
    ghost_north = pick_face(all_faces, own_lists[:, 3], 2)
    column_of = jnp.arange(cells, dtype=jnp.int32) % side
    shifted_right = jnp.concatenate([field[..., :1], field[..., :-1]], axis=-1)
    shifted_left = jnp.concatenate([field[..., 1:], field[..., -1:]], axis=-1)
    from_west = jnp.where(column_of == 0, jnp.repeat(ghost_west, side, axis=-1), shifted_right)
    from_east = jnp.where(
        column_of == side - 1, jnp.repeat(ghost_east, side, axis=-1), shifted_left
    )
    from_south = jnp.concatenate([ghost_south, field[..., : cells - side]], axis=-1)
    from_north = jnp.concatenate([field[..., side:], ghost_north], axis=-1)
    moved = field + 0.15 * (from_west + from_east + from_south + from_north - 4.0 * field)
    moved = moved - speed_u * (field - from_west) - speed_v * (field - from_south)
    return moved


def per_device(conc, wind_u, wind_v, emission, member_rate, column_top, settle_rate, neighbours):
    per_tile, members, bins, level_count, cells = conc.shape
    own_lists = lax.dynamic_slice_in_dim(neighbours, lax.axis_index("tile") * per_tile, per_tile, 0)
    inverse = make_inverse(settle_rate)
    levels_here = lax.axis_index("lev") * level_count + jnp.arange(level_count, dtype=jnp.int32)
    below = (levels_here[None, :] < column_top[:, None]).astype(jnp.float32)
    source = (
        emission[:, None, None, None, :]
        * member_rate[None, :, :, None, None]
        * below[None, :, None, :, None]
    )
    speed_u = wind_u.reshape(per_tile, 1, 1, level_count, cells)
    speed_v = wind_v.reshape(per_tile, 1, 1, level_count, cells)
    field = conc
    for turn_index in range(STEPS):
        field = field + source
        moved = horizontal(field, speed_u, speed_v, own_lists)
        columns = lax.all_to_all(moved, "lev", split_axis=4, concat_axis=3, tiled=True)
        settled = jnp.einsum("bkj,tmbjc->tmbkc", inverse, columns, precision=lax.Precision.HIGHEST)
        field = lax.all_to_all(settled, "lev", split_axis=3, concat_axis=4, tiled=True)
    return field


GRID_WIDTH = 8
HALO = 8
GROUP = 4


def lane_of(shape):
    return lax.broadcasted_iota(jnp.int32, shape, 1)


def pack_edges(tiles):
    group = ((lane_of(tiles[0].shape) + HALO) // (2 * HALO)) % GROUP
    packed = tiles[0]
    for i in range(1, len(tiles)):
        packed = jnp.where(group == i, pltpu.roll(tiles[i], 2 * HALO * i, 1), packed)
    return packed


def spread(main, edges, i):
    own = lane_of(main.shape) < TS
    turned = edges if i == 0 else pltpu.roll(edges, 128 - 2 * HALO * i, 1)
    even = jnp.where(own, main, pltpu.roll(turned, TS, 1))
    odd = jnp.where(own, pltpu.roll(main, TS, 1), turned)
    return even, odd


def window_kernel(
    tiles, levs, members,
    rate_hbm, top_hbm, settle_hbm, near_hbm, x_ref, u_ref, v_ref, em_ref,
    out_ref,
    rate_ref, top_ref, settle_ref, near_ref,
    inbuf, wind, halo, whalo, pick, eo, coef, emx, outbuf, solve,
    in_send, in_recv, near_recv, far_recv, wind_send, relay_send, em_send, em_recv, small_sem,
    whalo_send, whalo_recv, halo_send, halo_recv, out_send, out_recv, lev_ready, tile_ready,
):
    t = lax.axis_index("tile")
    d = lax.axis_index("lev")
    lev_peers = [lax.rem(d + o, levs) for o in range(1, levs)]
    tile_peers = [lax.rem(t + o, tiles) for o in range(1, tiles)]
    shape = (TS // 2, 128)

    half = levs // 2
    upper = d >= half

    barrier = pltpu.get_barrier_semaphore()
    for p in range(1, levs):
        @pl.when(d < p)
        def _():
            pl.semaphore_signal(barrier, inc=1, device_id={"lev": p})
    for p in range(1, tiles):
        @pl.when(t < p)
        def _():
            pl.semaphore_signal(barrier, inc=1, device_id={"tile": p})
    own_small = [
        pltpu.make_async_copy(src, dst, small_sem.at[i])
        for i, (src, dst) in enumerate(
            ((rate_hbm, rate_ref), (top_hbm, top_ref), (settle_hbm, settle_ref), (near_hbm, near_ref))
        )
    ]
    for copy in own_small:
        copy.start()

    @pl.when(d + t > 0)
    def _():
        pl.semaphore_wait(barrier, d + t)

    for p in range(levs - 1):
        @pl.when(p < d)
        def _():
            pl.semaphore_signal(lev_ready.at[d], inc=1, device_id={"lev": p})
    for p in range(tiles - 1):
        @pl.when(p < t)
        def _():
            pl.semaphore_signal(tile_ready, inc=1, device_id={"tile": p})

    def remote(src, dst, send_sem, recv_sem, where):
        return pltpu.make_async_remote_copy(
            src_ref=src, dst_ref=dst, send_sem=send_sem, recv_sem=recv_sem, device_id=where
        )

    def mine(p):
        return pl.ds(p * GROUP, GROUP)

    def arrived(ref, sem):
        pltpu.make_async_copy(ref, ref, sem).wait()

    def wind_copy(w, p, sem):
        return remote((u_ref, v_ref)[w], wind.at[d, w], wind_send, sem, {"lev": p})

    def send_winds(p):
        same = (d < half) if p < half else upper
        for w in range(2):
            @pl.when(same)
            def _():
                wind_copy(w, p, near_recv).start()
            if p in (half - 1, half):
                @pl.when(jnp.logical_not(same))
                def _():
                    wind_copy(w, p, far_recv).start()

    def in_copy(c, p):
        return remote(x_ref.at[c, mine(p)], inbuf.at[c, d], in_send, in_recv.at[c], {"lev": p})

    def out_copy(c, p):
        return remote(outbuf.at[c, p], out_ref.at[c, mine(d)], out_send, out_recv, {"lev": p})

    def wind_edge_copy(p):
        mine_now = whalo.at[t, pl.ds(0, 2)]
        return remote(mine_now, mine_now, whalo_send, whalo_recv, {"tile": p})

    def em_copy(p):
        return remote(em_ref, whalo.at[t, 2], em_send, em_recv, {"tile": p})

    def edge_copy(c, p):
        return remote(halo.at[c, t], halo.at[c, t], halo_send, halo_recv.at[c], {"tile": p})

    def own_in(c):
        return pltpu.make_async_copy(x_ref.at[c, mine(d)], inbuf.at[c, d], in_recv.at[c])

    def own_out(c):
        return pltpu.make_async_copy(outbuf.at[c, d], out_ref.at[c, mine(d)], out_recv)

    def start_in(c):
        for p in lev_peers:
            in_copy(c, p).start()
        own_in(c).start()

    for p in reversed(range(levs - 1)):
        @pl.when(p < d)
        def _():
            send_winds(p)
    for p in range(half):
        @pl.when(upper)
        def _():
            in_copy(0, p).start()
    for w in range(2):
        pltpu.make_async_copy((u_ref, v_ref)[w], wind.at[d, w], near_recv).start()
    pltpu.make_async_copy(em_ref, whalo.at[t, 2], em_recv).start()
    for p in range(1, levs):
        @pl.when(p > d)
        def _():
            pl.semaphore_wait(lev_ready.at[p], 1)
            send_winds(p)
            if p >= half:
                @pl.when(jnp.logical_not(upper))
                def _():
                    in_copy(0, p).start()

    @pl.when(t < tiles - 1)
    def _():
        pl.semaphore_wait(tile_ready, tiles - 1 - t)

    for p in tile_peers:
        em_copy(p).start()
    gates = ((half - 1, range(half - 1), half), (half, range(half + 1, levs), 0))
    for gate, others, first in gates:
        @pl.when(d == gate)
        def _():
            far = wind.at[pl.ds(first, half)]
            arrived(far, far_recv)
            for p in others:
                remote(far, far, relay_send, far_recv, {"lev": p}).start()
    for p in range(levs):
        @pl.when((p != d) & ((p >= half) == upper))
        def _():
            in_copy(0, p).start()
    own_in(0).start()
    arrived(wind.at[pl.ds(0, half)], near_recv)

    @pl.when((d != half) & (d != half - 1))
    def _():
        arrived(wind.at[pl.ds(0, half)], far_recv)

    for w in range(2):
        whalo[t, w] = pack_edges([wind[k, w] for k in range(levs)])
    for p in tile_peers:
        wind_edge_copy(p).start()
    start_in(1)

    for copy in own_small:
        copy.wait()

    for i in range(GROUP):
        for k in range(levs):
            q = 1.0 / (1.0 + jnp.full((8, 128), settle_ref[k, d * GROUP + i], jnp.float32))
            solve[i, k, 0] = q
            if k + 1 < levs:
                solve[i, k, 1] = q * settle_ref[k + 1, d * GROUP + i]
            else:
                solve[i, k, 1] = jnp.zeros((8, 128), jnp.float32)

    lane = lane_of(shape)
    row = lax.broadcasted_iota(jnp.int32, shape, 0)
    west, east = near_ref[0, t], near_ref[1, t]
    has_west = jnp.where(west >= 0, 1.0, 0.0)
    has_east = jnp.where(east >= 0, 1.0, 0.0)
    east_lane = lax.rem(lane_of((8, 128)), 2 * HALO) < HALO
    for p in range(tiles):
        pick[p] = jnp.where(
            east_lane,
            jnp.full((8, 128), jnp.where(east == p, 1.0, 0.0), jnp.float32),
            jnp.full((8, 128), jnp.where(west == p, 1.0, 0.0), jnp.float32),
        )

    def wide(value):
        return jnp.concatenate([value] * (shape[0] // 8), axis=0)

    def edges_of(packed):
        total = wide(pick[0]) * packed(0)
        for p in range(1, tiles):
            total = total + wide(pick[p]) * packed(p)
        return total

    def gather_edges(c):
        arrived(inbuf.at[c], in_recv.at[c])

        @pl.when(c + 2 < members)
        def _():
            start_in(c + 2)

        def pack_level(k, carry):
            halo[c, t, k] = pack_edges([inbuf[c, k, i] for i in range(GROUP)])
            return carry

        lax.fori_loop(0, levs, pack_level, 0)
        for p in tile_peers:
            edge_copy(c, p).start()

    def coefficients():
        arrived(whalo.at[pl.ds(0, tiles - 1), pl.ds(0, 2)], whalo_recv)
        arrived(whalo.at[:, 2], em_recv)
        live = jnp.where(lane < TS, 1.0, 0.0)
        live = jnp.where((lane >= TS) & (lane < TS + HALO), has_east, live)
        live = jnp.where(lane >= 128 - HALO, has_west, live)
        edges = [edges_of(lambda p, w=w: whalo[p, w]) for w in range(3)]
        even, odd = spread(whalo[t, 2], edges[2], 0)
        emx[0] = even * live
        emx[1] = odd * live
        emx[2] = 0.15 * live
        emx[3] = jnp.where(row == TS // 2 - 1, 0.0, 0.15 * live)
        for k in range(levs):
            us = spread(wind[k, 0], edges[0], k)
            vs = spread(wind[k, 1], edges[1], k)
            for e in range(2):
                coef[k, e, 0] = (0.4 - us[e] - vs[e]) * live
                coef[k, e, 1] = (0.15 + us[e]) * live
                south = (0.15 + vs[e]) * live
                coef[k, e, 2] = jnp.where(row == 0, 0.0, south) if e == 0 else south

    def run(c):
        arrived(halo.at[c, pl.ds(0, tiles - 1)], halo_recv.at[c])

        def build(k, carry):
            edges = edges_of(lambda p: halo[c, p, k])
            for i in range(GROUP):
                even, odd = spread(inbuf[c, k, i], edges, i)
                eo[k, i, 0] = even
                eo[k, i, 1] = odd
            return carry

        lax.fori_loop(0, levs, build, 0)

        def one_bin(i, carry):
            rate = rate_ref[c, d * GROUP + i]
            above_even = above_odd = None
            for k in reversed(range(levs)):
                s = jnp.where(k < top_ref[c], rate, 0.0)
                even = eo[k, i, 0] + emx[0] * s
                odd = eo[k, i, 1] + emx[1] * s
                moved_even = (
                    coef[k, 0, 0] * even
                    + coef[k, 0, 1] * pltpu.roll(even, 1, 1)
                    + coef[k, 0, 2] * pltpu.roll(odd, 1, 0)
                    + emx[2] * (pltpu.roll(even, 127, 1) + odd)
                )
                moved_odd = (
                    coef[k, 1, 0] * odd
                    + coef[k, 1, 1] * pltpu.roll(odd, 1, 1)
                    + coef[k, 1, 2] * even
                    + emx[2] * pltpu.roll(odd, 127, 1)
                    + emx[3] * pltpu.roll(even, shape[0] - 1, 0)
                )
                q = wide(solve[i, k, 0])
                new_even, new_odd = q * moved_even, q * moved_odd
                if above_even is not None:
                    g = wide(solve[i, k, 1])
                    new_even = new_even + g * above_even
                    new_odd = new_odd + g * above_odd
                eo[k, i, 0] = new_even
                eo[k, i, 1] = new_odd
                above_even, above_odd = new_even, new_odd
            return carry

        def one_step(step, carry):
            return lax.fori_loop(0, GROUP, one_bin, carry, unroll=2)

        lax.fori_loop(0, STEPS, one_step, 0)

        def join(k, carry):
            for i in range(GROUP):
                outbuf[c, k, i] = jnp.where(lane < TS, eo[k, i, 0], pltpu.roll(eo[k, i, 1], TS, 1))
            return carry

        lax.fori_loop(0, levs, join, 0)
        for p in lev_peers:
            out_copy(c, p).start()
        own_out(c).start()

    gather_edges(0)
    coefficients()

    def one_member(c, carry):
        @pl.when(c + 1 < members)
        def _():
            gather_edges(c + 1)

        run(c)
        return carry

    lax.fori_loop(0, members, one_member, 0)

    arrived(out_ref, out_recv)
    arrived(inbuf.at[:, pl.ds(0, levs - 1)], in_send)
    arrived(wind.at[pl.ds(0, half)], wind_send)
    for gate, others, first in gates:
        @pl.when(d == gate)
        def _():
            for p in others:
                arrived(wind.at[pl.ds(0, half)], relay_send)
    arrived(whalo.at[pl.ds(0, tiles - 1), pl.ds(0, 2)], whalo_send)
    arrived(whalo.at[pl.ds(0, tiles - 1), 2], em_send)
    arrived(halo.at[:, pl.ds(0, tiles - 1)], halo_send)
    arrived(outbuf.at[:, pl.ds(0, levs - 1)], out_send)


def window(tiles, levs, conc, wind_u, wind_v, emission, member_rate, column_top, settle_rate, neighbours):
    members, bins = conc.shape[1], conc.shape[2]
    tile = (TS // 2, 128)
    x = conc.reshape((members, bins) + tile)
    f32 = jnp.float32
    dma = pltpu.SemaphoreType.DMA
    hbm = pl.BlockSpec(memory_space=pltpu.HBM)
    out = pl.pallas_call(
        functools.partial(window_kernel, tiles, levs, members),
        out_shape=pltpu.VMEM(x.shape, f32),
        in_specs=[hbm] * 8,
        out_specs=pl.BlockSpec(memory_space=pltpu.VMEM),
        scratch_shapes=[
            pltpu.SMEM(member_rate.shape, f32),
            pltpu.SMEM(column_top.shape, jnp.int32),
            pltpu.SMEM(settle_rate.shape[::-1], f32),
            pltpu.SMEM(neighbours.shape[::-1], jnp.int32),
            pltpu.VMEM((members, levs, GROUP) + tile, f32),
            pltpu.VMEM((levs, 2) + tile, f32),
            pltpu.VMEM((members, tiles, levs) + tile, f32),
            pltpu.VMEM((tiles, 3) + tile, f32),
            pltpu.VMEM((tiles, 8, 128), f32),
            pltpu.VMEM((levs, GROUP, 2) + tile, f32),
            pltpu.VMEM((levs, 2, 3) + tile, f32),
            pltpu.VMEM((4,) + tile, f32),
            pltpu.VMEM((members, levs, GROUP) + tile, f32),
            pltpu.VMEM((GROUP, levs, 2, 8, 128), f32),
            dma,
            dma((members,)),
            dma,
            dma,
            dma,
            dma,
            dma,
            dma,
            dma((4,)),
            dma,
            dma,
            dma,
            dma((members,)),
            dma,
            dma,
            pltpu.SemaphoreType.REGULAR((levs,)),
            pltpu.SemaphoreType.REGULAR,
        ],
        compiler_params=pltpu.CompilerParams(
            collective_id=0, has_side_effects=True, vmem_limit_bytes=58 * 1024 * 1024
        ),
        name="window",
    )(
        member_rate, column_top, settle_rate.T, neighbours.T,
        x, wind_u.reshape(tile), wind_v.reshape(tile), emission.reshape(tile),
    )
    return out.reshape(conc.shape)


def choose(mesh):
    tiles, levs = mesh.shape["tile"], mesh.shape["lev"]

    def body(conc, *rest):
        per_tile, members, bins, level_count, cells = conc.shape
        one_row = tiles * per_tile == GRID_WIDTH
        fits = per_tile == 1 and level_count == 1 and bins == levs * GROUP and levs in (2, GROUP) and members > 1
        if one_row and fits and cells == TS * TS and TS == 64 and STEPS <= HALO:
            return window(tiles, levs, conc, *rest)
        return per_device(conc, *rest)

    return body


def solution(mesh):
    return jax.shard_map(
        choose(mesh),
        mesh=mesh,
        in_specs=(
            P("tile", None, None, "lev", None),
            P("tile", "lev", None),
            P("tile", "lev", None),
            P("tile", None),
            P(),
            P(),
            P(),
            P(),
        ),
        out_specs=P("tile", None, None, "lev", None),
        check_vma=False,
    )
```

```python
import functools
import jax
import jax.numpy as jnp
from jax import lax
from jax.experimental import pallas as pl
from jax.experimental.pallas import tpu as pltpu
from jax.sharding import PartitionSpec as P

TS = 64
STEPS = 6


def make_inverse(settle_rate):
    levels = settle_rate.shape[1]
    ident = jnp.eye(levels, dtype=settle_rate.dtype)
    diag_all = 1.0 + settle_rate
    next_rate = jnp.concatenate([settle_rate[:, 1:], jnp.zeros_like(settle_rate[:, :1])], axis=1)

    def back_step(carry, inputs):
        unit_row, rate_next, diag_here = inputs
        row_now = (unit_row[None, :] + rate_next[:, None] * carry) / diag_here[:, None]
        return (row_now, row_now)

    start = jnp.zeros((settle_rate.shape[0], levels), dtype=settle_rate.dtype)
    unused, stacked = lax.scan(back_step, start, (ident, next_rate.T, diag_all.T), reverse=True)
    return jnp.transpose(stacked, (1, 0, 2))


def pick_face(all_faces, index, which):
    chosen = all_faces[jnp.clip(index, 0, all_faces.shape[0] - 1), which]
    valid = (index >= 0).astype(jnp.float32)
    return chosen * valid[:, None, None, None, None]


def horizontal(field, speed_u, speed_v, own_lists):
    per_tile, members, bins, levels, cells = field.shape
    side = TS
    west_face = field[..., 0::side]
    east_face = field[..., side - 1 :: side]
    south_face = field[..., :side]
    north_face = field[..., cells - side :]
    edge_stack = jnp.stack([west_face, east_face, south_face, north_face], axis=1)
    edge_flat = edge_stack.reshape(per_tile, 4, members, bins, levels * side)
    gathered = lax.all_gather(edge_flat, "tile", axis=0, tiled=True)
    all_faces = gathered.reshape(gathered.shape[0], 4, members, bins, levels, side)
    ghost_west = pick_face(all_faces, own_lists[:, 0], 1)
    ghost_east = pick_face(all_faces, own_lists[:, 1], 0)
    ghost_south = pick_face(all_faces, own_lists[:, 2], 3)
    ghost_north = pick_face(all_faces, own_lists[:, 3], 2)
    column_of = jnp.arange(cells, dtype=jnp.int32) % side
    shifted_right = jnp.concatenate([field[..., :1], field[..., :-1]], axis=-1)
    shifted_left = jnp.concatenate([field[..., 1:], field[..., -1:]], axis=-1)
    from_west = jnp.where(column_of == 0, jnp.repeat(ghost_west, side, axis=-1), shifted_right)
    from_east = jnp.where(
        column_of == side - 1, jnp.repeat(ghost_east, side, axis=-1), shifted_left
    )
    from_south = jnp.concatenate([ghost_south, field[..., : cells - side]], axis=-1)
    from_north = jnp.concatenate([field[..., side:], ghost_north], axis=-1)
    moved = field + 0.15 * (from_west + from_east + from_south + from_north - 4.0 * field)
    moved = moved - speed_u * (field - from_west) - speed_v * (field - from_south)
    return moved


def per_device(conc, wind_u, wind_v, emission, member_rate, column_top, settle_rate, neighbours):
    per_tile, members, bins, level_count, cells = conc.shape
    own_lists = lax.dynamic_slice_in_dim(neighbours, lax.axis_index("tile") * per_tile, per_tile, 0)
    inverse = make_inverse(settle_rate)
    levels_here = lax.axis_index("lev") * level_count + jnp.arange(level_count, dtype=jnp.int32)
    below = (levels_here[None, :] < column_top[:, None]).astype(jnp.float32)
    source = (
        emission[:, None, None, None, :]
        * member_rate[None, :, :, None, None]
        * below[None, :, None, :, None]
    )
    speed_u = wind_u.reshape(per_tile, 1, 1, level_count, cells)
    speed_v = wind_v.reshape(per_tile, 1, 1, level_count, cells)
    field = conc
    for turn_index in range(STEPS):
        field = field + source
        moved = horizontal(field, speed_u, speed_v, own_lists)
        columns = lax.all_to_all(moved, "lev", split_axis=4, concat_axis=3, tiled=True)
        settled = jnp.einsum("bkj,tmbjc->tmbkc", inverse, columns, precision=lax.Precision.HIGHEST)
        field = lax.all_to_all(settled, "lev", split_axis=3, concat_axis=4, tiled=True)
    return field


GRID_WIDTH = 8
HALO = 8
GROUP = 4


def lane_of(shape):
    return lax.broadcasted_iota(jnp.int32, shape, 1)


def pack_edges(tiles):
    group = ((lane_of(tiles[0].shape) + HALO) // (2 * HALO)) % GROUP
    packed = tiles[0]
    for i in range(1, len(tiles)):
        packed = jnp.where(group == i, pltpu.roll(tiles[i], 2 * HALO * i, 1), packed)
    return packed


def spread(main, edges, i):
    own = lane_of(main.shape) < TS
    turned = edges if i == 0 else pltpu.roll(edges, 128 - 2 * HALO * i, 1)
    even = jnp.where(own, main, pltpu.roll(turned, TS, 1))
    odd = jnp.where(own, pltpu.roll(main, TS, 1), turned)
    return even, odd


def window_kernel(
    tiles, levs, members,
    rate_hbm, top_hbm, settle_hbm, near_hbm, x_ref, u_ref, v_ref, em_ref,
    out_ref,
    rate_ref, top_ref, settle_ref, near_ref,
    inbuf, wind, halo, whalo, pick, eo, coef, emx, outbuf, solve,
    in_send, in_recv, near_recv, far_recv, wind_send, relay_send, em_send, em_recv, small_sem,
    whalo_send, whalo_recv, halo_send, halo_recv, out_send, out_recv, lev_ready, tile_ready,
):
    t = lax.axis_index("tile")
    d = lax.axis_index("lev")
    lev_peers = [lax.rem(d + o, levs) for o in range(1, levs)]
    tile_peers = [lax.rem(t + o, tiles) for o in range(1, tiles)]
    shape = (TS // 2, 128)

    half = levs // 2
    upper = d >= half

    barrier = pltpu.get_barrier_semaphore()
    for p in range(1, levs):
        @pl.when(d < p)
        def _():
            pl.semaphore_signal(barrier, inc=1, device_id={"lev": p})
    own_small = [
        pltpu.make_async_copy(src, dst, small_sem.at[i])
        for i, (src, dst) in enumerate(
            ((rate_hbm, rate_ref), (top_hbm, top_ref), (settle_hbm, settle_ref), (near_hbm, near_ref))
        )
    ]
    for copy in own_small:
        copy.start()

    @pl.when(d > 0)
    def _():
        pl.semaphore_wait(barrier, d)

    for p in range(levs - 1):
        @pl.when(p < d)
        def _():
            pl.semaphore_signal(lev_ready.at[d], inc=1, device_id={"lev": p})

    def remote(src, dst, send_sem, recv_sem, where):
        return pltpu.make_async_remote_copy(
            src_ref=src, dst_ref=dst, send_sem=send_sem, recv_sem=recv_sem, device_id=where
        )

    def mine(p):
        return pl.ds(p * GROUP, GROUP)

    def arrived(ref, sem):
        pltpu.make_async_copy(ref, ref, sem).wait()

    def wind_copy(w, p, sem):
        return remote((u_ref, v_ref)[w], wind.at[d, w], wind_send, sem, {"lev": p})

    def send_winds(p):
        same = (d < half) if p < half else upper
        for w in range(2):
            @pl.when(same)
            def _():
                wind_copy(w, p, near_recv).start()
            if p in (half - 1, half):
                @pl.when(jnp.logical_not(same))
                def _():
                    wind_copy(w, p, far_recv).start()

    def in_copy(c, p):
        return remote(x_ref.at[c, mine(p)], inbuf.at[c, d], in_send, in_recv.at[c], {"lev": p})

    def out_copy(c, p):
        return remote(outbuf.at[c, p], out_ref.at[c, mine(d)], out_send, out_recv, {"lev": p})

    def wind_edge_copy(p):
        mine_now = whalo.at[t, pl.ds(0, 2)]
        return remote(mine_now, mine_now, whalo_send, whalo_recv, {"tile": p})

    def em_copy(p):
        return remote(em_ref, whalo.at[t, 2], em_send, em_recv, {"tile": p})

    def edge_copy(c, p):
        return remote(halo.at[c, t], halo.at[c, t], halo_send, halo_recv.at[c], {"tile": p})

    def own_in(c):
        return pltpu.make_async_copy(x_ref.at[c, mine(d)], inbuf.at[c, d], in_recv.at[c])

    def own_out(c):
        return pltpu.make_async_copy(outbuf.at[c, d], out_ref.at[c, mine(d)], out_recv)

    def start_in(c):
        for p in lev_peers:
            in_copy(c, p).start()
        own_in(c).start()

    for p in reversed(range(levs - 1)):
        @pl.when(p < d)
        def _():
            send_winds(p)
    for p in range(half):
        @pl.when(upper)
        def _():
            in_copy(0, p).start()
    for w in range(2):
        pltpu.make_async_copy((u_ref, v_ref)[w], wind.at[d, w], near_recv).start()
    pltpu.make_async_copy(em_ref, whalo.at[t, 2], em_recv).start()
    for p in range(1, levs):
        @pl.when(p > d)
        def _():
            pl.semaphore_wait(lev_ready.at[p], 1)
            send_winds(p)
            if p >= half:
                @pl.when(jnp.logical_not(upper))
                def _():
                    in_copy(0, p).start()

    @pl.when(d == 0)
    def _():
        for p in tile_peers:
            pl.semaphore_signal(barrier, inc=1, device_id={"tile": p})
        pl.semaphore_wait(barrier, tiles - 1)
        for p in range(1, levs):
            pl.semaphore_signal(tile_ready, inc=1, device_id={"lev": p})

    gates = ((half - 1, range(half - 1), half), (half, range(half + 1, levs), 0))
    for gate, others, first in gates:
        @pl.when(d == gate)
        def _():
            far = wind.at[pl.ds(first, half)]
            arrived(far, far_recv)
            for p in others:
                remote(far, far, relay_send, far_recv, {"lev": p}).start()
    for p in range(levs):
        @pl.when((p != d) & ((p >= half) == upper))
        def _():
            in_copy(0, p).start()
    own_in(0).start()
    arrived(wind.at[pl.ds(0, half)], near_recv)

    @pl.when((d != half) & (d != half - 1))
    def _():
        arrived(wind.at[pl.ds(0, half)], far_recv)

    @pl.when(d > 0)
    def _():
        pl.semaphore_wait(tile_ready, 1)

    for p in tile_peers:
        em_copy(p).start()
    for w in range(2):
        whalo[t, w] = pack_edges([wind[k, w] for k in range(levs)])
    for p in tile_peers:
        wind_edge_copy(p).start()
    start_in(1)

    for copy in own_small:
        copy.wait()

    for i in range(GROUP):
        for k in range(levs):
            q = 1.0 / (1.0 + jnp.full((8, 128), settle_ref[k, d * GROUP + i], jnp.float32))
            solve[i, k, 0] = q
            if k + 1 < levs:
                solve[i, k, 1] = q * settle_ref[k + 1, d * GROUP + i]
            else:
                solve[i, k, 1] = jnp.zeros((8, 128), jnp.float32)

    lane = lane_of(shape)
    row = lax.broadcasted_iota(jnp.int32, shape, 0)
    west, east = near_ref[0, t], near_ref[1, t]
    has_west = jnp.where(west >= 0, 1.0, 0.0)
    has_east = jnp.where(east >= 0, 1.0, 0.0)
    east_lane = lax.rem(lane_of((8, 128)), 2 * HALO) < HALO
    for p in range(tiles):
        pick[p] = jnp.where(
            east_lane,
            jnp.full((8, 128), jnp.where(east == p, 1.0, 0.0), jnp.float32),
            jnp.full((8, 128), jnp.where(west == p, 1.0, 0.0), jnp.float32),
        )

    def wide(value):
        return jnp.concatenate([value] * (shape[0] // 8), axis=0)

    def edges_of(packed):
        total = wide(pick[0]) * packed(0)
        for p in range(1, tiles):
            total = total + wide(pick[p]) * packed(p)
        return total

    def gather_edges(c):
        arrived(inbuf.at[c], in_recv.at[c])

        @pl.when(c + 2 < members)
        def _():
            start_in(c + 2)

        def pack_level(k, carry):
            halo[c, t, k] = pack_edges([inbuf[c, k, i] for i in range(GROUP)])
            return carry

        lax.fori_loop(0, levs, pack_level, 0)
        for p in tile_peers:
            edge_copy(c, p).start()

    def coefficients():
        arrived(whalo.at[pl.ds(0, tiles - 1), pl.ds(0, 2)], whalo_recv)
        arrived(whalo.at[:, 2], em_recv)
        live = jnp.where(lane < TS, 1.0, 0.0)
        live = jnp.where((lane >= TS) & (lane < TS + HALO), has_east, live)
        live = jnp.where(lane >= 128 - HALO, has_west, live)
        edges = [edges_of(lambda p, w=w: whalo[p, w]) for w in range(3)]
        even, odd = spread(whalo[t, 2], edges[2], 0)
        emx[0] = even * live
        emx[1] = odd * live
        emx[2] = 0.15 * live
        emx[3] = jnp.where(row == TS // 2 - 1, 0.0, 0.15 * live)
        for k in range(levs):
            us = spread(wind[k, 0], edges[0], k)
            vs = spread(wind[k, 1], edges[1], k)
            for e in range(2):
                coef[k, e, 0] = (0.4 - us[e] - vs[e]) * live
                coef[k, e, 1] = (0.15 + us[e]) * live
                south = (0.15 + vs[e]) * live
                coef[k, e, 2] = jnp.where(row == 0, 0.0, south) if e == 0 else south

    def run(c):
        arrived(halo.at[c, pl.ds(0, tiles - 1)], halo_recv.at[c])

        def build(k, carry):
            edges = edges_of(lambda p: halo[c, p, k])
            for i in range(GROUP):
                even, odd = spread(inbuf[c, k, i], edges, i)
                eo[k, i, 0] = even
                eo[k, i, 1] = odd
            return carry

        lax.fori_loop(0, levs, build, 0)

        def one_bin(i, carry):
            rate = rate_ref[c, d * GROUP + i]
            above_even = above_odd = None
            for k in reversed(range(levs)):
                s = jnp.where(k < top_ref[c], rate, 0.0)
                even = eo[k, i, 0] + emx[0] * s
                odd = eo[k, i, 1] + emx[1] * s
                moved_even = (
                    coef[k, 0, 0] * even
                    + coef[k, 0, 1] * pltpu.roll(even, 1, 1)
                    + coef[k, 0, 2] * pltpu.roll(odd, 1, 0)
                    + emx[2] * (pltpu.roll(even, 127, 1) + odd)
                )
                moved_odd = (
                    coef[k, 1, 0] * odd
                    + coef[k, 1, 1] * pltpu.roll(odd, 1, 1)
                    + coef[k, 1, 2] * even
                    + emx[2] * pltpu.roll(odd, 127, 1)
                    + emx[3] * pltpu.roll(even, shape[0] - 1, 0)
                )
                q = wide(solve[i, k, 0])
                new_even, new_odd = q * moved_even, q * moved_odd
                if above_even is not None:
                    g = wide(solve[i, k, 1])
                    new_even = new_even + g * above_even
                    new_odd = new_odd + g * above_odd
                eo[k, i, 0] = new_even
                eo[k, i, 1] = new_odd
                above_even, above_odd = new_even, new_odd
            return carry

        def one_step(step, carry):
            return lax.fori_loop(0, GROUP, one_bin, carry, unroll=2)

        lax.fori_loop(0, STEPS, one_step, 0)

        def join(k, carry):
            for i in range(GROUP):
                outbuf[c, k, i] = jnp.where(lane < TS, eo[k, i, 0], pltpu.roll(eo[k, i, 1], TS, 1))
            return carry

        lax.fori_loop(0, levs, join, 0)
        for p in lev_peers:
            out_copy(c, p).start()
        own_out(c).start()

    gather_edges(0)
    coefficients()

    def one_member(c, carry):
        @pl.when(c + 1 < members)
        def _():
            gather_edges(c + 1)

        run(c)
        return carry

    lax.fori_loop(0, members, one_member, 0)

    arrived(out_ref, out_recv)
    arrived(inbuf.at[:, pl.ds(0, levs - 1)], in_send)
    arrived(wind.at[pl.ds(0, half)], wind_send)
    for gate, others, first in gates:
        @pl.when(d == gate)
        def _():
            for p in others:
                arrived(wind.at[pl.ds(0, half)], relay_send)
    arrived(whalo.at[pl.ds(0, tiles - 1), pl.ds(0, 2)], whalo_send)
    arrived(whalo.at[pl.ds(0, tiles - 1), 2], em_send)
    arrived(halo.at[:, pl.ds(0, tiles - 1)], halo_send)
    arrived(outbuf.at[:, pl.ds(0, levs - 1)], out_send)


def window(tiles, levs, conc, wind_u, wind_v, emission, member_rate, column_top, settle_rate, neighbours):
    members, bins = conc.shape[1], conc.shape[2]
    tile = (TS // 2, 128)
    x = conc.reshape((members, bins) + tile)
    f32 = jnp.float32
    dma = pltpu.SemaphoreType.DMA
    hbm = pl.BlockSpec(memory_space=pltpu.HBM)
    out = pl.pallas_call(
        functools.partial(window_kernel, tiles, levs, members),
        out_shape=pltpu.VMEM(x.shape, f32),
        in_specs=[hbm] * 8,
        out_specs=pl.BlockSpec(memory_space=pltpu.VMEM),
        scratch_shapes=[
            pltpu.SMEM(member_rate.shape, f32),
            pltpu.SMEM(column_top.shape, jnp.int32),
            pltpu.SMEM(settle_rate.shape[::-1], f32),
            pltpu.SMEM(neighbours.shape[::-1], jnp.int32),
            pltpu.VMEM((members, levs, GROUP) + tile, f32),
            pltpu.VMEM((levs, 2) + tile, f32),
            pltpu.VMEM((members, tiles, levs) + tile, f32),
            pltpu.VMEM((tiles, 3) + tile, f32),
            pltpu.VMEM((tiles, 8, 128), f32),
            pltpu.VMEM((levs, GROUP, 2) + tile, f32),
            pltpu.VMEM((levs, 2, 3) + tile, f32),
            pltpu.VMEM((4,) + tile, f32),
            pltpu.VMEM((members, levs, GROUP) + tile, f32),
            pltpu.VMEM((GROUP, levs, 2, 8, 128), f32),
            dma,
            dma((members,)),
            dma,
            dma,
            dma,
            dma,
            dma,
            dma,
            dma((4,)),
            dma,
            dma,
            dma,
            dma((members,)),
            dma,
            dma,
            pltpu.SemaphoreType.REGULAR((levs,)),
            pltpu.SemaphoreType.REGULAR,
        ],
        compiler_params=pltpu.CompilerParams(
            collective_id=0, has_side_effects=True, vmem_limit_bytes=58 * 1024 * 1024
        ),
        name="window",
    )(
        member_rate, column_top, settle_rate.T, neighbours.T,
        x, wind_u.reshape(tile), wind_v.reshape(tile), emission.reshape(tile),
    )
    return out.reshape(conc.shape)


def choose(mesh):
    tiles, levs = mesh.shape["tile"], mesh.shape["lev"]

    def body(conc, *rest):
        per_tile, members, bins, level_count, cells = conc.shape
        one_row = tiles * per_tile == GRID_WIDTH
        fits = per_tile == 1 and level_count == 1 and bins == levs * GROUP and levs in (2, GROUP) and members > 1
        if one_row and fits and cells == TS * TS and TS == 64 and STEPS <= HALO:
            return window(tiles, levs, conc, *rest)
        return per_device(conc, *rest)

    return body


def solution(mesh):
    return jax.shard_map(
        choose(mesh),
        mesh=mesh,
        in_specs=(
            P("tile", None, None, "lev", None),
            P("tile", "lev", None),
            P("tile", "lev", None),
            P("tile", None),
            P(),
            P(),
            P(),
            P(),
        ),
        out_specs=P("tile", None, None, "lev", None),
        check_vma=False,
    )
```

```python
import functools
import jax
import jax.numpy as jnp
from jax import lax
from jax.experimental import pallas as pl
from jax.experimental.pallas import tpu as pltpu
from jax.sharding import PartitionSpec as P

TS = 64
STEPS = 6


def make_inverse(settle_rate):
    levels = settle_rate.shape[1]
    ident = jnp.eye(levels, dtype=settle_rate.dtype)
    diag_all = 1.0 + settle_rate
    next_rate = jnp.concatenate([settle_rate[:, 1:], jnp.zeros_like(settle_rate[:, :1])], axis=1)

    def back_step(carry, inputs):
        unit_row, rate_next, diag_here = inputs
        row_now = (unit_row[None, :] + rate_next[:, None] * carry) / diag_here[:, None]
        return (row_now, row_now)

    start = jnp.zeros((settle_rate.shape[0], levels), dtype=settle_rate.dtype)
    unused, stacked = lax.scan(back_step, start, (ident, next_rate.T, diag_all.T), reverse=True)
    return jnp.transpose(stacked, (1, 0, 2))


def pick_face(all_faces, index, which):
    chosen = all_faces[jnp.clip(index, 0, all_faces.shape[0] - 1), which]
    valid = (index >= 0).astype(jnp.float32)
    return chosen * valid[:, None, None, None, None]


def horizontal(field, speed_u, speed_v, own_lists):
    per_tile, members, bins, levels, cells = field.shape
    side = TS
    west_face = field[..., 0::side]
    east_face = field[..., side - 1 :: side]
    south_face = field[..., :side]
    north_face = field[..., cells - side :]
    edge_stack = jnp.stack([west_face, east_face, south_face, north_face], axis=1)
    edge_flat = edge_stack.reshape(per_tile, 4, members, bins, levels * side)
    gathered = lax.all_gather(edge_flat, "tile", axis=0, tiled=True)
    all_faces = gathered.reshape(gathered.shape[0], 4, members, bins, levels, side)
    ghost_west = pick_face(all_faces, own_lists[:, 0], 1)
    ghost_east = pick_face(all_faces, own_lists[:, 1], 0)
    ghost_south = pick_face(all_faces, own_lists[:, 2], 3)
    ghost_north = pick_face(all_faces, own_lists[:, 3], 2)
    column_of = jnp.arange(cells, dtype=jnp.int32) % side
    shifted_right = jnp.concatenate([field[..., :1], field[..., :-1]], axis=-1)
    shifted_left = jnp.concatenate([field[..., 1:], field[..., -1:]], axis=-1)
    from_west = jnp.where(column_of == 0, jnp.repeat(ghost_west, side, axis=-1), shifted_right)
    from_east = jnp.where(
        column_of == side - 1, jnp.repeat(ghost_east, side, axis=-1), shifted_left
    )
    from_south = jnp.concatenate([ghost_south, field[..., : cells - side]], axis=-1)
    from_north = jnp.concatenate([field[..., side:], ghost_north], axis=-1)
    moved = field + 0.15 * (from_west + from_east + from_south + from_north - 4.0 * field)
    moved = moved - speed_u * (field - from_west) - speed_v * (field - from_south)
    return moved


def per_device(conc, wind_u, wind_v, emission, member_rate, column_top, settle_rate, neighbours):
    per_tile, members, bins, level_count, cells = conc.shape
    own_lists = lax.dynamic_slice_in_dim(neighbours, lax.axis_index("tile") * per_tile, per_tile, 0)
    inverse = make_inverse(settle_rate)
    levels_here = lax.axis_index("lev") * level_count + jnp.arange(level_count, dtype=jnp.int32)
    below = (levels_here[None, :] < column_top[:, None]).astype(jnp.float32)
    source = (
        emission[:, None, None, None, :]
        * member_rate[None, :, :, None, None]
        * below[None, :, None, :, None]
    )
    speed_u = wind_u.reshape(per_tile, 1, 1, level_count, cells)
    speed_v = wind_v.reshape(per_tile, 1, 1, level_count, cells)
    field = conc
    for turn_index in range(STEPS):
        field = field + source
        moved = horizontal(field, speed_u, speed_v, own_lists)
        columns = lax.all_to_all(moved, "lev", split_axis=4, concat_axis=3, tiled=True)
        settled = jnp.einsum("bkj,tmbjc->tmbkc", inverse, columns, precision=lax.Precision.HIGHEST)
        field = lax.all_to_all(settled, "lev", split_axis=3, concat_axis=4, tiled=True)
    return field


GRID_WIDTH = 8
HALO = 8
GROUP = 4


def lane_of(shape):
    return lax.broadcasted_iota(jnp.int32, shape, 1)


def pack_edges(tiles):
    group = ((lane_of(tiles[0].shape) + HALO) // (2 * HALO)) % GROUP
    packed = tiles[0]
    for i in range(1, len(tiles)):
        packed = jnp.where(group == i, pltpu.roll(tiles[i], 2 * HALO * i, 1), packed)
    return packed


def spread(main, edges, i):
    own = lane_of(main.shape) < TS
    turned = edges if i == 0 else pltpu.roll(edges, 128 - 2 * HALO * i, 1)
    even = jnp.where(own, main, pltpu.roll(turned, TS, 1))
    odd = jnp.where(own, pltpu.roll(main, TS, 1), turned)
    return even, odd


def window_kernel(
    tiles, levs, members,
    rate_hbm, top_hbm, settle_hbm, near_hbm, x_ref, u_ref, v_ref, em_ref,
    out_ref,
    rate_ref, top_ref, settle_ref, near_ref,
    inbuf, wind, halo, whalo, pick, eo, coef, emx, outbuf, solve,
    lev_send, in_recv, near_recv, far_recv, wind_send, small_sem,
    whalo_send, whalo_recv, halo_send, halo_recv, out_recv, lev_ready, tile_ready,
):
    t = lax.axis_index("tile")
    d = lax.axis_index("lev")
    lev_peers = [lax.rem(d + o, levs) for o in range(1, levs)]
    tile_peers = [lax.rem(t + o, tiles) for o in range(1, tiles)]
    shape = (TS // 2, 128)

    half = levs // 2
    upper = d >= half

    barrier = pltpu.get_barrier_semaphore()
    for p in range(1, levs):
        @pl.when(d < p)
        def _():
            pl.semaphore_signal(barrier, inc=1, device_id={"lev": p})
    own_small = [
        pltpu.make_async_copy(src, dst, small_sem.at[i])
        for i, (src, dst) in enumerate(
            ((rate_hbm, rate_ref), (top_hbm, top_ref), (settle_hbm, settle_ref), (near_hbm, near_ref))
        )
    ]
    for copy in own_small:
        copy.start()

    @pl.when(d > 0)
    def _():
        pl.semaphore_wait(barrier, d)

    for p in range(levs - 1):
        @pl.when(p < d)
        def _():
            pl.semaphore_signal(lev_ready.at[d - 1], inc=1, device_id={"lev": p})

    def remote(src, dst, send_sem, recv_sem, where):
        return pltpu.make_async_remote_copy(
            src_ref=src, dst_ref=dst, send_sem=send_sem, recv_sem=recv_sem, device_id=where
        )

    def mine(p):
        return pl.ds(p * GROUP, GROUP)

    def arrived(ref, sem):
        pltpu.make_async_copy(ref, ref, sem).wait()

    def wind_copy(w, p, sem):
        return remote((u_ref, v_ref)[w], wind.at[d, w], wind_send, sem, {"lev": p})

    def send_winds(p):
        same = (d < half) if p < half else upper
        for w in range(2):
            @pl.when(same)
            def _():
                wind_copy(w, p, near_recv).start()
            if p in (half - 1, half):
                @pl.when(jnp.logical_not(same))
                def _():
                    wind_copy(w, p, far_recv).start()

    def in_copy(c, p):
        return remote(x_ref.at[c, mine(p)], inbuf.at[c, d], lev_send, in_recv.at[c], {"lev": p})

    def out_copy(c, p):
        return remote(outbuf.at[c, p], out_ref.at[c, mine(d)], lev_send, out_recv, {"lev": p})

    def wind_edge_copy(p):
        mine_now = whalo.at[t, pl.ds(0, 2)]
        return remote(mine_now, mine_now, whalo_send, whalo_recv, {"tile": p})

    def em_copy(p):
        return remote(em_ref, whalo.at[t, 2], whalo_send, whalo_recv, {"tile": p})

    def edge_copy(c, p):
        return remote(halo.at[c, t], halo.at[c, t], halo_send, halo_recv.at[c], {"tile": p})

    def own_in(c):
        return pltpu.make_async_copy(x_ref.at[c, mine(d)], inbuf.at[c, d], in_recv.at[c])

    def own_out(c):
        return pltpu.make_async_copy(outbuf.at[c, d], out_ref.at[c, mine(d)], out_recv)

    def start_in(c):
        for p in lev_peers:
            in_copy(c, p).start()
        own_in(c).start()

    for p in reversed(range(levs - 1)):
        @pl.when(p < d)
        def _():
            send_winds(p)
    for p in range(half):
        @pl.when(upper)
        def _():
            in_copy(0, p).start()
    for w in range(2):
        pltpu.make_async_copy((u_ref, v_ref)[w], wind.at[d, w], near_recv).start()
    pltpu.make_async_copy(em_ref, whalo.at[t, 2], near_recv).start()
    for p in range(1, levs):
        @pl.when(p > d)
        def _():
            pl.semaphore_wait(lev_ready.at[p - 1], 1)
            send_winds(p)
            if p >= half:
                @pl.when(jnp.logical_not(upper))
                def _():
                    in_copy(0, p).start()

    @pl.when(d == 0)
    def _():
        for p in tile_peers:
            pl.semaphore_signal(barrier, inc=1, device_id={"tile": p})
        pl.semaphore_wait(barrier, tiles - 1)
        for p in range(1, levs):
            pl.semaphore_signal(tile_ready, inc=1, device_id={"lev": p})

    gates = ((half - 1, range(half - 1), half), (half, range(half + 1, levs), 0))
    for gate, others, first in gates:
        @pl.when(d == gate)
        def _():
            far = wind.at[pl.ds(first, half)]
            arrived(far, far_recv)
            for p in others:
                remote(far, far, wind_send, far_recv, {"lev": p}).start()
    for p in range(levs):
        @pl.when((p != d) & ((p >= half) == upper))
        def _():
            in_copy(0, p).start()
    own_in(0).start()
    arrived(whalo.at[pl.ds(0, 2 * half + 1), 0], near_recv)

    @pl.when((d != half) & (d != half - 1))
    def _():
        arrived(wind.at[pl.ds(0, half)], far_recv)

    @pl.when(d > 0)
    def _():
        pl.semaphore_wait(tile_ready, 1)

    for p in tile_peers:
        em_copy(p).start()
    for w in range(2):
        whalo[t, w] = pack_edges([wind[k, w] for k in range(levs)])
    for p in tile_peers:
        wind_edge_copy(p).start()
    start_in(1)

    for copy in own_small:
        copy.wait()

    for i in range(GROUP):
        for k in range(levs):
            q = 1.0 / (1.0 + jnp.full((8, 128), settle_ref[k, d * GROUP + i], jnp.float32))
            solve[i, k, 0] = q
            if k + 1 < levs:
                solve[i, k, 1] = q * settle_ref[k + 1, d * GROUP + i]
            else:
                solve[i, k, 1] = jnp.zeros((8, 128), jnp.float32)

    lane = lane_of(shape)
    row = lax.broadcasted_iota(jnp.int32, shape, 0)
    west, east = near_ref[0, t], near_ref[1, t]
    has_west = jnp.where(west >= 0, 1.0, 0.0)
    has_east = jnp.where(east >= 0, 1.0, 0.0)
    east_lane = lax.rem(lane_of((8, 128)), 2 * HALO) < HALO
    for p in range(tiles):
        pick[p] = jnp.where(
            east_lane,
            jnp.full((8, 128), jnp.where(east == p, 1.0, 0.0), jnp.float32),
            jnp.full((8, 128), jnp.where(west == p, 1.0, 0.0), jnp.float32),
        )

    def wide(value):
        return jnp.concatenate([value] * (shape[0] // 8), axis=0)

    def edges_of(packed):
        total = wide(pick[0]) * packed(0)
        for p in range(1, tiles):
            total = total + wide(pick[p]) * packed(p)
        return total

    def gather_edges(c):
        arrived(inbuf.at[c], in_recv.at[c])

        def pack_level(k, carry):
            halo[c, t, k] = pack_edges([inbuf[c, k, i] for i in range(GROUP)])
            return carry

        lax.fori_loop(0, levs, pack_level, 0)
        for p in tile_peers:
            edge_copy(c, p).start()

    def coefficients():
        arrived(whalo.at[pl.ds(0, tiles - 1)], whalo_recv)
        live = jnp.where(lane < TS, 1.0, 0.0)
        live = jnp.where((lane >= TS) & (lane < TS + HALO), has_east, live)
        live = jnp.where(lane >= 128 - HALO, has_west, live)
        edges = [edges_of(lambda p, w=w: whalo[p, w]) for w in range(3)]
        even, odd = spread(whalo[t, 2], edges[2], 0)
        emx[0] = even * live
        emx[1] = odd * live
        emx[2] = 0.15 * live
        emx[3] = jnp.where(row == TS // 2 - 1, 0.0, 0.15 * live)
        for k in range(levs):
            us = spread(wind[k, 0], edges[0], k)
            vs = spread(wind[k, 1], edges[1], k)
            for e in range(2):
                coef[k, e, 0] = (0.4 - us[e] - vs[e]) * live
                coef[k, e, 1] = (0.15 + us[e]) * live
                south = (0.15 + vs[e]) * live
                coef[k, e, 2] = jnp.where(row == 0, 0.0, south) if e == 0 else south

    def run(c):
        arrived(halo.at[c, pl.ds(0, tiles - 1)], halo_recv.at[c])

        def build(k, carry):
            edges = edges_of(lambda p: halo[c, p, k])
            for i in range(GROUP):
                even, odd = spread(inbuf[c, k, i], edges, i)
                eo[k, i, 0] = even
                eo[k, i, 1] = odd
            return carry

        lax.fori_loop(0, levs, build, 0)

        def one_bin(i, carry):
            rate = rate_ref[c, d * GROUP + i]
            above_even = above_odd = None
            for k in reversed(range(levs)):
                s = jnp.where(k < top_ref[c], rate, 0.0)
                even = eo[k, i, 0] + emx[0] * s
                odd = eo[k, i, 1] + emx[1] * s
                moved_even = (
                    coef[k, 0, 0] * even
                    + coef[k, 0, 1] * pltpu.roll(even, 1, 1)
                    + coef[k, 0, 2] * pltpu.roll(odd, 1, 0)
                    + emx[2] * (pltpu.roll(even, 127, 1) + odd)
                )
                moved_odd = (
                    coef[k, 1, 0] * odd
                    + coef[k, 1, 1] * pltpu.roll(odd, 1, 1)
                    + coef[k, 1, 2] * even
                    + emx[2] * pltpu.roll(odd, 127, 1)
                    + emx[3] * pltpu.roll(even, shape[0] - 1, 0)
                )
                q = wide(solve[i, k, 0])
                new_even, new_odd = q * moved_even, q * moved_odd
                if above_even is not None:
                    g = wide(solve[i, k, 1])
                    new_even = new_even + g * above_even
                    new_odd = new_odd + g * above_odd
                eo[k, i, 0] = new_even
                eo[k, i, 1] = new_odd
                above_even, above_odd = new_even, new_odd
            return carry

        def one_step(step, carry):
            return lax.fori_loop(0, GROUP, one_bin, carry, unroll=2)

        lax.fori_loop(0, STEPS, one_step, 0)

        def join(k, carry):
            for i in range(GROUP):
                outbuf[c, k, i] = jnp.where(lane < TS, eo[k, i, 0], pltpu.roll(eo[k, i, 1], TS, 1))
            return carry

        lax.fori_loop(0, levs, join, 0)
        for p in lev_peers:
            out_copy(c, p).start()
        own_out(c).start()

    gather_edges(0)
    start_in(2)
    coefficients()
    start_in(3)

    def one_member(c, carry):
        @pl.when(c + 1 < members)
        def _():
            gather_edges(c + 1)

        run(c)
        return carry

    lax.fori_loop(0, members, one_member, 0)

    arrived(out_ref, out_recv)
    arrived(halo.at[:, pl.ds(0, 2 * (levs - 1))], lev_send)

    @pl.when((d == half) | (d == half - 1))
    def _():
        arrived(wind.at[pl.ds(0, 2 * half)], wind_send)

    @pl.when((d != half) & (d != half - 1))
    def _():
        arrived(wind.at[pl.ds(0, half)], wind_send)

    arrived(whalo.at[pl.ds(0, tiles - 1)], whalo_send)
    arrived(halo.at[:, pl.ds(0, tiles - 1)], halo_send)


def window(tiles, levs, conc, wind_u, wind_v, emission, member_rate, column_top, settle_rate, neighbours):
    members, bins = conc.shape[1], conc.shape[2]
    tile = (TS // 2, 128)
    x = conc.reshape((members, bins) + tile)
    f32 = jnp.float32
    dma = pltpu.SemaphoreType.DMA
    hbm = pl.BlockSpec(memory_space=pltpu.HBM)
    out = pl.pallas_call(
        functools.partial(window_kernel, tiles, levs, members),
        out_shape=pltpu.VMEM(x.shape, f32),
        in_specs=[hbm] * 8,
        out_specs=pl.BlockSpec(memory_space=pltpu.VMEM),
        scratch_shapes=[
            pltpu.SMEM(member_rate.shape, f32),
            pltpu.SMEM(column_top.shape, jnp.int32),
            pltpu.SMEM(settle_rate.shape[::-1], f32),
            pltpu.SMEM(neighbours.shape[::-1], jnp.int32),
            pltpu.VMEM((members, levs, GROUP) + tile, f32),
            pltpu.VMEM((levs, 2) + tile, f32),
            pltpu.VMEM((members, tiles, levs) + tile, f32),
            pltpu.VMEM((tiles, 3) + tile, f32),
            pltpu.VMEM((tiles, 8, 128), f32),
            pltpu.VMEM((levs, GROUP, 2) + tile, f32),
            pltpu.VMEM((levs, 2, 3) + tile, f32),
            pltpu.VMEM((4,) + tile, f32),
            pltpu.VMEM((members, levs, GROUP) + tile, f32),
            pltpu.VMEM((GROUP, levs, 2, 8, 128), f32),
            dma,
            dma((members,)),
            dma,
            dma,
            dma,
            dma((4,)),
            dma,
            dma,
            dma,
            dma((members,)),
            dma,
            pltpu.SemaphoreType.REGULAR((levs - 1,)),
            pltpu.SemaphoreType.REGULAR,
        ],
        compiler_params=pltpu.CompilerParams(
            collective_id=0, has_side_effects=True, vmem_limit_bytes=58 * 1024 * 1024
        ),
        name="window",
    )(
        member_rate, column_top, settle_rate.T, neighbours.T,
        x, wind_u.reshape(tile), wind_v.reshape(tile), emission.reshape(tile),
    )
    return out.reshape(conc.shape)


def choose(mesh):
    tiles, levs = mesh.shape["tile"], mesh.shape["lev"]

    def body(conc, *rest):
        per_tile, members, bins, level_count, cells = conc.shape
        one_row = tiles * per_tile == GRID_WIDTH
        fits = per_tile == 1 and level_count == 1 and bins == levs * GROUP and levs == GROUP and members > 1
        if one_row and fits and cells == TS * TS and TS == 64 and STEPS <= HALO:
            return window(tiles, levs, conc, *rest)
        return per_device(conc, *rest)

    return body


def solution(mesh):
    return jax.shard_map(
        choose(mesh),
        mesh=mesh,
        in_specs=(
            P("tile", None, None, "lev", None),
            P("tile", "lev", None),
            P("tile", "lev", None),
            P("tile", None),
            P(),
            P(),
            P(),
            P(),
        ),
        out_specs=P("tile", None, None, "lev", None),
        check_vma=False,
    )
```

```python
import functools
import jax
import jax.numpy as jnp
from jax import lax
from jax.experimental import pallas as pl
from jax.experimental.pallas import tpu as pltpu
from jax.sharding import PartitionSpec as P

TS = 64
STEPS = 6


def make_inverse(settle_rate):
    levels = settle_rate.shape[1]
    ident = jnp.eye(levels, dtype=settle_rate.dtype)
    diag_all = 1.0 + settle_rate
    next_rate = jnp.concatenate([settle_rate[:, 1:], jnp.zeros_like(settle_rate[:, :1])], axis=1)

    def back_step(carry, inputs):
        unit_row, rate_next, diag_here = inputs
        row_now = (unit_row[None, :] + rate_next[:, None] * carry) / diag_here[:, None]
        return (row_now, row_now)

    start = jnp.zeros((settle_rate.shape[0], levels), dtype=settle_rate.dtype)
    unused, stacked = lax.scan(back_step, start, (ident, next_rate.T, diag_all.T), reverse=True)
    return jnp.transpose(stacked, (1, 0, 2))


def pick_face(all_faces, index, which):
    chosen = all_faces[jnp.clip(index, 0, all_faces.shape[0] - 1), which]
    valid = (index >= 0).astype(jnp.float32)
    return chosen * valid[:, None, None, None, None]


def horizontal(field, speed_u, speed_v, own_lists):
    per_tile, members, bins, levels, cells = field.shape
    side = TS
    west_face = field[..., 0::side]
    east_face = field[..., side - 1 :: side]
    south_face = field[..., :side]
    north_face = field[..., cells - side :]
    edge_stack = jnp.stack([west_face, east_face, south_face, north_face], axis=1)
    edge_flat = edge_stack.reshape(per_tile, 4, members, bins, levels * side)
    gathered = lax.all_gather(edge_flat, "tile", axis=0, tiled=True)
    all_faces = gathered.reshape(gathered.shape[0], 4, members, bins, levels, side)
    ghost_west = pick_face(all_faces, own_lists[:, 0], 1)
    ghost_east = pick_face(all_faces, own_lists[:, 1], 0)
    ghost_south = pick_face(all_faces, own_lists[:, 2], 3)
    ghost_north = pick_face(all_faces, own_lists[:, 3], 2)
    column_of = jnp.arange(cells, dtype=jnp.int32) % side
    shifted_right = jnp.concatenate([field[..., :1], field[..., :-1]], axis=-1)
    shifted_left = jnp.concatenate([field[..., 1:], field[..., -1:]], axis=-1)
    from_west = jnp.where(column_of == 0, jnp.repeat(ghost_west, side, axis=-1), shifted_right)
    from_east = jnp.where(
        column_of == side - 1, jnp.repeat(ghost_east, side, axis=-1), shifted_left
    )
    from_south = jnp.concatenate([ghost_south, field[..., : cells - side]], axis=-1)
    from_north = jnp.concatenate([field[..., side:], ghost_north], axis=-1)
    moved = field + 0.15 * (from_west + from_east + from_south + from_north - 4.0 * field)
    moved = moved - speed_u * (field - from_west) - speed_v * (field - from_south)
    return moved


def per_device(conc, wind_u, wind_v, emission, member_rate, column_top, settle_rate, neighbours):
    per_tile, members, bins, level_count, cells = conc.shape
    own_lists = lax.dynamic_slice_in_dim(neighbours, lax.axis_index("tile") * per_tile, per_tile, 0)
    inverse = make_inverse(settle_rate)
    levels_here = lax.axis_index("lev") * level_count + jnp.arange(level_count, dtype=jnp.int32)
    below = (levels_here[None, :] < column_top[:, None]).astype(jnp.float32)
    source = (
        emission[:, None, None, None, :]
        * member_rate[None, :, :, None, None]
        * below[None, :, None, :, None]
    )
    speed_u = wind_u.reshape(per_tile, 1, 1, level_count, cells)
    speed_v = wind_v.reshape(per_tile, 1, 1, level_count, cells)
    field = conc
    for turn_index in range(STEPS):
        field = field + source
        moved = horizontal(field, speed_u, speed_v, own_lists)
        columns = lax.all_to_all(moved, "lev", split_axis=4, concat_axis=3, tiled=True)
        settled = jnp.einsum("bkj,tmbjc->tmbkc", inverse, columns, precision=lax.Precision.HIGHEST)
        field = lax.all_to_all(settled, "lev", split_axis=3, concat_axis=4, tiled=True)
    return field


GRID_WIDTH = 8
HALO = 8
GROUP = 4


def lane_of(shape):
    return lax.broadcasted_iota(jnp.int32, shape, 1)


def pack_edges(tiles):
    group = ((lane_of(tiles[0].shape) + HALO) // (2 * HALO)) % GROUP
    packed = tiles[0]
    for i in range(1, len(tiles)):
        packed = jnp.where(group == i, pltpu.roll(tiles[i], 2 * HALO * i, 1), packed)
    return packed


def spread(main, edges, i):
    own = lane_of(main.shape) < TS
    turned = edges if i == 0 else pltpu.roll(edges, 128 - 2 * HALO * i, 1)
    even = jnp.where(own, main, pltpu.roll(turned, TS, 1))
    odd = jnp.where(own, pltpu.roll(main, TS, 1), turned)
    return even, odd


def window_kernel(
    tiles, levs, members,
    rate_hbm, top_hbm, settle_hbm, near_hbm, x_ref, u_ref, v_ref, em_ref,
    out_ref,
    rate_ref, top_ref, settle_ref, near_ref,
    inbuf, wind, halo, whalo, pick, eo, coef, emx, outbuf, solve,
    lev_send, in_recv, near_recv, far_recv, wind_send, small_sem,
    whalo_send, whalo_recv, halo_send, halo_recv, out_recv, lev_ready, tile_ready,
):
    t = lax.axis_index("tile")
    d = lax.axis_index("lev")
    lev_peers = [lax.rem(d + o, levs) for o in range(1, levs)]
    tile_peers = [lax.rem(t + o, tiles) for o in range(1, tiles)]
    shape = (TS // 2, 128)

    half = levs // 2
    upper = d >= half

    barrier = pltpu.get_barrier_semaphore()
    for p in range(1, levs):
        @pl.when(d < p)
        def _():
            pl.semaphore_signal(barrier, inc=1, device_id={"lev": p})
    own_small = [
        pltpu.make_async_copy(src, dst, small_sem.at[i])
        for i, (src, dst) in enumerate(
            ((rate_hbm, rate_ref), (top_hbm, top_ref), (settle_hbm, settle_ref), (near_hbm, near_ref))
        )
    ]
    for copy in own_small:
        copy.start()

    @pl.when(d > 0)
    def _():
        pl.semaphore_wait(barrier, d)

    for p in range(levs - 1):
        @pl.when(p < d)
        def _():
            pl.semaphore_signal(lev_ready.at[d - 1], inc=1, device_id={"lev": p})

    def remote(src, dst, send_sem, recv_sem, where):
        return pltpu.make_async_remote_copy(
            src_ref=src, dst_ref=dst, send_sem=send_sem, recv_sem=recv_sem, device_id=where
        )

    def mine(p):
        return pl.ds(p * GROUP, GROUP)

    def arrived(ref, sem):
        pltpu.make_async_copy(ref, ref, sem).wait()

    def wind_copy(w, p, sem):
        return remote((u_ref, v_ref)[w], wind.at[d, w], wind_send, sem, {"lev": p})

    def send_winds(p):
        same = (d < half) if p < half else upper
        for w in range(2):
            @pl.when(same)
            def _():
                wind_copy(w, p, near_recv).start()
            if p in (half - 1, half):
                @pl.when(jnp.logical_not(same))
                def _():
                    wind_copy(w, p, far_recv).start()

    def in_copy(c, p):
        return remote(x_ref.at[c, mine(p)], inbuf.at[c, d], lev_send, in_recv.at[c], {"lev": p})

    def out_copy(c, p):
        return remote(outbuf.at[c, p], out_ref.at[c, mine(d)], lev_send, out_recv, {"lev": p})

    def wind_edge_copy(p):
        mine_now = whalo.at[t, pl.ds(0, 2)]
        return remote(mine_now, mine_now, whalo_send, whalo_recv, {"tile": p})

    def em_copy(p):
        return remote(em_ref, whalo.at[t, 2], whalo_send, whalo_recv, {"tile": p})

    def edge_copy(c, p):
        return remote(halo.at[c, t], halo.at[c, t], halo_send, halo_recv.at[c], {"tile": p})

    def own_in(c):
        return pltpu.make_async_copy(x_ref.at[c, mine(d)], inbuf.at[c, d], in_recv.at[c])

    def own_out(c):
        return pltpu.make_async_copy(outbuf.at[c, d], out_ref.at[c, mine(d)], out_recv)

    def start_in(c):
        for p in lev_peers:
            in_copy(c, p).start()
        own_in(c).start()

    for p in reversed(range(levs - 1)):
        @pl.when(p < d)
        def _():
            send_winds(p)
    for p in range(half):
        @pl.when(upper)
        def _():
            in_copy(0, p).start()
    for w in range(2):
        pltpu.make_async_copy((u_ref, v_ref)[w], wind.at[d, w], near_recv).start()
    pltpu.make_async_copy(em_ref, whalo.at[t, 2], near_recv).start()
    for p in range(1, levs):
        @pl.when(p > d)
        def _():
            pl.semaphore_wait(lev_ready.at[p - 1], 1)
            send_winds(p)
            if p >= half:
                @pl.when(jnp.logical_not(upper))
                def _():
                    in_copy(0, p).start()

    @pl.when(d == 0)
    def _():
        for p in tile_peers:
            pl.semaphore_signal(barrier, inc=1, device_id={"tile": p})
        pl.semaphore_wait(barrier, tiles - 1)
        for p in range(1, levs):
            pl.semaphore_signal(tile_ready, inc=1, device_id={"lev": p})

    gates = ((half - 1, range(half - 1), half), (half, range(half + 1, levs), 0))
    for gate, others, first in gates:
        @pl.when(d == gate)
        def _():
            far = wind.at[pl.ds(first, half)]
            arrived(far, far_recv)
            for p in others:
                remote(far, far, wind_send, far_recv, {"lev": p}).start()
    for p in range(levs):
        @pl.when((p != d) & ((p >= half) == upper))
        def _():
            in_copy(0, p).start()
    own_in(0).start()
    arrived(whalo.at[pl.ds(0, 2 * half + 1), 0], near_recv)

    @pl.when((d != half) & (d != half - 1))
    def _():
        arrived(wind.at[pl.ds(0, half)], far_recv)

    @pl.when(d > 0)
    def _():
        pl.semaphore_wait(tile_ready, 1)

    for p in tile_peers:
        em_copy(p).start()
    for w in range(2):
        whalo[t, w] = pack_edges([wind[k, w] for k in range(levs)])
    for p in tile_peers:
        wind_edge_copy(p).start()
    start_in(1)

    for copy in own_small:
        copy.wait()

    for i in range(GROUP):
        for k in range(levs):
            q = 1.0 / (1.0 + jnp.full((8, 128), settle_ref[k, d * GROUP + i], jnp.float32))
            solve[i, k, 0] = q
            if k + 1 < levs:
                solve[i, k, 1] = q * settle_ref[k + 1, d * GROUP + i]
            else:
                solve[i, k, 1] = jnp.zeros((8, 128), jnp.float32)

    lane = lane_of(shape)
    row = lax.broadcasted_iota(jnp.int32, shape, 0)
    west, east = near_ref[0, t], near_ref[1, t]
    has_west = jnp.where(west >= 0, 1.0, 0.0)
    has_east = jnp.where(east >= 0, 1.0, 0.0)
    east_lane = lax.rem(lane_of((8, 128)), 2 * HALO) < HALO
    for p in range(tiles):
        pick[p] = jnp.where(
            east_lane,
            jnp.full((8, 128), jnp.where(east == p, 1.0, 0.0), jnp.float32),
            jnp.full((8, 128), jnp.where(west == p, 1.0, 0.0), jnp.float32),
        )

    def wide(value):
        return jnp.concatenate([value] * (shape[0] // 8), axis=0)

    def edges_of(packed):
        total = wide(pick[0]) * packed(0)
        for p in range(1, tiles):
            total = total + wide(pick[p]) * packed(p)
        return total

    def gather_edges(c):
        arrived(inbuf.at[c], in_recv.at[c])

        def pack_level(k, carry):
            halo[c, t, k] = pack_edges([inbuf[c, k, i] for i in range(GROUP)])
            return carry

        lax.fori_loop(0, levs, pack_level, 0)
        for p in tile_peers:
            edge_copy(c, p).start()

    def coefficients():
        arrived(whalo.at[pl.ds(0, tiles - 1)], whalo_recv)
        live = jnp.where(lane < TS, 1.0, 0.0)
        live = jnp.where((lane >= TS) & (lane < TS + HALO), has_east, live)
        live = jnp.where(lane >= 128 - HALO, has_west, live)
        edges = [edges_of(lambda p, w=w: whalo[p, w]) for w in range(3)]
        even, odd = spread(whalo[t, 2], edges[2], 0)
        emx[0] = even * live
        emx[1] = odd * live
        emx[2] = 0.15 * live
        emx[3] = jnp.where(row == TS // 2 - 1, 0.0, 0.15 * live)
        for k in range(levs):
            us = spread(wind[k, 0], edges[0], k)
            vs = spread(wind[k, 1], edges[1], k)
            for e in range(2):
                coef[k, e, 0] = (0.4 - us[e] - vs[e]) * live
                coef[k, e, 1] = (0.15 + us[e]) * live
                south = (0.15 + vs[e]) * live
                coef[k, e, 2] = jnp.where(row == 0, 0.0, south) if e == 0 else south

    def run(c):
        arrived(halo.at[c, pl.ds(0, tiles - 1)], halo_recv.at[c])

        def build(k, carry):
            edges = edges_of(lambda p: halo[c, p, k])
            for i in range(GROUP):
                even, odd = spread(inbuf[c, k, i], edges, i)
                eo[k, i, 0] = even
                eo[k, i, 1] = odd
            return carry

        lax.fori_loop(0, levs, build, 0)

        def one_bin(i, carry):
            rate = rate_ref[c, d * GROUP + i]
            above_even = above_odd = None
            for k in reversed(range(levs)):
                s = jnp.where(k < top_ref[c], rate, 0.0)
                even = eo[k, i, 0] + emx[0] * s
                odd = eo[k, i, 1] + emx[1] * s
                moved_even = (
                    coef[k, 0, 0] * even
                    + coef[k, 0, 1] * pltpu.roll(even, 1, 1)
                    + coef[k, 0, 2] * pltpu.roll(odd, 1, 0)
                    + emx[2] * (pltpu.roll(even, 127, 1) + odd)
                )
                moved_odd = (
                    coef[k, 1, 0] * odd
                    + coef[k, 1, 1] * pltpu.roll(odd, 1, 1)
                    + coef[k, 1, 2] * even
                    + emx[2] * pltpu.roll(odd, 127, 1)
                    + emx[3] * pltpu.roll(even, shape[0] - 1, 0)
                )
                q = wide(solve[i, k, 0])
                new_even, new_odd = q * moved_even, q * moved_odd
                if above_even is not None:
                    g = wide(solve[i, k, 1])
                    new_even = new_even + g * above_even
                    new_odd = new_odd + g * above_odd
                eo[k, i, 0] = new_even
                eo[k, i, 1] = new_odd
                above_even, above_odd = new_even, new_odd
            return carry

        def one_step(step, carry):
            return lax.fori_loop(0, GROUP, one_bin, carry, unroll=2)

        lax.fori_loop(0, STEPS, one_step, 0)

        def join(k, carry):
            for i in range(GROUP):
                outbuf[c, k, i] = jnp.where(lane < TS, eo[k, i, 0], pltpu.roll(eo[k, i, 1], TS, 1))
            return carry

        lax.fori_loop(0, levs, join, 0)
        own_out(c).start()
        for p in range(levs):
            @pl.when(p != d)
            def _():
                out_copy(c, p).start()

    gather_edges(0)
    start_in(2)
    coefficients()
    start_in(3)

    def one_member(c, carry):
        @pl.when(c + 1 < members)
        def _():
            gather_edges(c + 1)

        run(c)
        return carry

    lax.fori_loop(0, members, one_member, 0)

    arrived(out_ref, out_recv)
    arrived(halo.at[:, pl.ds(0, 2 * (levs - 1))], lev_send)

    @pl.when((d == half) | (d == half - 1))
    def _():
        arrived(wind.at[pl.ds(0, 2 * half)], wind_send)

    @pl.when((d != half) & (d != half - 1))
    def _():
        arrived(wind.at[pl.ds(0, half)], wind_send)

    arrived(whalo.at[pl.ds(0, tiles - 1)], whalo_send)
    arrived(halo.at[:, pl.ds(0, tiles - 1)], halo_send)


def window(tiles, levs, conc, wind_u, wind_v, emission, member_rate, column_top, settle_rate, neighbours):
    members, bins = conc.shape[1], conc.shape[2]
    tile = (TS // 2, 128)
    x = conc.reshape((members, bins) + tile)
    f32 = jnp.float32
    dma = pltpu.SemaphoreType.DMA
    hbm = pl.BlockSpec(memory_space=pltpu.HBM)
    out = pl.pallas_call(
        functools.partial(window_kernel, tiles, levs, members),
        out_shape=pltpu.VMEM(x.shape, f32),
        in_specs=[hbm] * 8,
        out_specs=pl.BlockSpec(memory_space=pltpu.VMEM),
        scratch_shapes=[
            pltpu.SMEM(member_rate.shape, f32),
            pltpu.SMEM(column_top.shape, jnp.int32),
            pltpu.SMEM(settle_rate.shape[::-1], f32),
            pltpu.SMEM(neighbours.shape[::-1], jnp.int32),
            pltpu.VMEM((members, levs, GROUP) + tile, f32),
            pltpu.VMEM((levs, 2) + tile, f32),
            pltpu.VMEM((members, tiles, levs) + tile, f32),
            pltpu.VMEM((tiles, 3) + tile, f32),
            pltpu.VMEM((tiles, 8, 128), f32),
            pltpu.VMEM((levs, GROUP, 2) + tile, f32),
            pltpu.VMEM((levs, 2, 3) + tile, f32),
            pltpu.VMEM((4,) + tile, f32),
            pltpu.VMEM((members, levs, GROUP) + tile, f32),
            pltpu.VMEM((GROUP, levs, 2, 8, 128), f32),
            dma,
            dma((members,)),
            dma,
            dma,
            dma,
            dma((4,)),
            dma,
            dma,
            dma,
            dma((members,)),
            dma,
            pltpu.SemaphoreType.REGULAR((levs - 1,)),
            pltpu.SemaphoreType.REGULAR,
        ],
        compiler_params=pltpu.CompilerParams(
            collective_id=0, has_side_effects=True, vmem_limit_bytes=58 * 1024 * 1024
        ),
        name="window",
    )(
        member_rate, column_top, settle_rate.T, neighbours.T,
        x, wind_u.reshape(tile), wind_v.reshape(tile), emission.reshape(tile),
    )
    return out.reshape(conc.shape)


def choose(mesh):
    tiles, levs = mesh.shape["tile"], mesh.shape["lev"]

    def body(conc, *rest):
        per_tile, members, bins, level_count, cells = conc.shape
        one_row = tiles * per_tile == GRID_WIDTH
        fits = per_tile == 1 and level_count == 1 and bins == levs * GROUP and levs == GROUP and members > 1
        if one_row and fits and cells == TS * TS and TS == 64 and STEPS <= HALO:
            return window(tiles, levs, conc, *rest)
        return per_device(conc, *rest)

    return body


def solution(mesh):
    return jax.shard_map(
        choose(mesh),
        mesh=mesh,
        in_specs=(
            P("tile", None, None, "lev", None),
            P("tile", "lev", None),
            P("tile", "lev", None),
            P("tile", None),
            P(),
            P(),
            P(),
            P(),
        ),
        out_specs=P("tile", None, None, "lev", None),
        check_vma=False,
    )
```
